512 devices in a mesh: freq: 8 (over z), trow: 4 (over x), tcol: 16 (over y, core).
Axes of the slice: x: 4, y: 8, z: 8, core: 2. Of those that a mesh axis runs over, the one named last changes fastest.
Arguments:
- traces: bfloat16 [16, 16, 1024, 1024], P('freq', 'tcol', 'trow'), may hold values from -6 to 6
- u_bases: bfloat16 [8, 32, 64, 2, 32, 256], P('freq', 'trow', 'tcol'), may hold values from -0.09375 to 0.09375
- v_bases: bfloat16 [8, 32, 64, 2, 32, 256], P('freq', 'trow', 'tcol'), may hold values from -0.25 to 0.25
- ranks: int32 [8, 32, 64], P('freq', 'trow', 'tcol'), may hold values from 1 to 32, as said below
- observed: float32 [8, 2, 16, 8192], P('freq', None, None, 'trow'), may hold values from -6 to 6
Outputs:
- residual: float32 [8, 2, 16, 8192], P('freq', None, None, 'trow')
- gradient: bfloat16 [16, 16, 1024, 1024], P('freq', 'tcol', 'trow')
The draws below stay inside these ranges and needn't reach their ends.
Inputs may be any that keep to these rules, and one draw needn't show every extreme that they name: `ranks`: each tile's rank at each frequency; at every frequency some tile has rank 32.
All inputs are finite; a program needn't handle non-finite values.
Results may differ from the reference program's by a relative error of at most 0.023.
Values may be sent and summed in bfloat16 or wider, within the bound.
No kernel may reach another device: no remote copies, remote signals or barrier semaphores. Data moves between devices by JAX's collectives and lax.ppermute only.
A program may use at most 64 MiB of HBM per device.

```python
import math
import jax
import jax.numpy as jnp
from jax import lax

TILE = 256
RMAX = 32
NT = 1024
FIRST_BIN = 40
NV = 16
NF = 8
NTR = 32
NTC = 64
NR = 8192
NS = 16384
SBLK = 16
SPOS = 1024


def draw_ranks(key, part):
    key = jax.random.fold_in(key, 7)
    keys = jax.random.split(key, 5)
    shape = (NF, NTR, NTC)
    busy_column_list = jax.random.randint(keys[0], (NTC,), 0, 4) == 0
    heavy_pick = jax.random.randint(keys[1], shape, 0, 2) == 0
    light_ranks = jax.random.randint(keys[2], shape, 1, RMAX // 2 + 1)
    heavy_ranks = jax.random.randint(keys[3], shape, RMAX // 2 + 1, RMAX + 1)
    rank_values = jnp.where(busy_column_list[None, None, :] & heavy_pick, heavy_ranks, light_ranks)
    chosen = jax.random.randint(keys[4], (NF,), 0, NTR * NTC)
    tile_index = jnp.arange(NTR * NTC, dtype=jnp.int32).reshape(NTR, NTC)
    rank_values = jnp.where(tile_index[None, :, :] == chosen[:, None, None], RMAX, rank_values)
    return rank_values.astype(jnp.int32)


def level_of(stream_key, dims, cuts, least, high):
    loudness = 1.0
    for position, parts in cuts:
        heights = jax.random.uniform(jax.random.fold_in(jax.random.fold_in(stream_key, 6), position), (parts,), jnp.float32, least / len(cuts), high / len(cuts))
        loudness = loudness * jnp.repeat(jnp.exp(heights), dims[position] // parts).reshape((-1,) + (1,) * (len(dims) - 1 - position))
    return loudness


def noise(rng, extent, spread, reach, cuts=(), kind=jnp.bfloat16):
    drawn = jax.random.normal(rng, extent, jnp.float32) * spread
    if len(cuts) > 0:
        drawn = level_of(rng, extent, cuts, -0.22, 0.18) * drawn
    return jnp.clip(drawn, min=-reach, max=reach).astype(kind)


def setup_inputs(seed: int = 0) -> dict:
    key_of = jax.random.split(jax.random.key(seed), 6)
    traces = noise(key_of[0], (NV, SBLK, SPOS, NT), 1.0, 6.0, ((0, 8), (1, 16), (2, 4)))
    u_bases = noise(key_of[1], (NF, NTR, NTC, 2, RMAX, TILE), (2 * RMAX * NTC) ** -0.5, 0.09375, ((0, 8), (1, 4), (2, 16)))
    v_bases = noise(key_of[2], (NF, NTR, NTC, 2, RMAX, TILE), (2 * TILE) ** -0.5, 0.25, ((0, 8), (1, 4), (2, 16)))
    ranks = draw_ranks(jax.random.fold_in(key_of[5], 71), 0)
    observed = noise(key_of[4], (NF, 2, NV, NR), 1.0, 6.0, ((0, 8), (3, 4)), jnp.float32)
    return dict(traces=traces, u_bases=u_bases, v_bases=v_bases, ranks=ranks, observed=observed)


def dft_table(freq_count, first_bin, trace_len):
    freq_bins = first_bin + jnp.arange(freq_count, dtype=jnp.int32)
    time_steps = jnp.arange(trace_len, dtype=jnp.int32)
    phase_index = freq_bins[:, None] * time_steps[None, :] % trace_len
    angles = phase_index.astype(jnp.float32) * (2.0 * math.pi / trace_len)
    return jnp.stack([jnp.cos(angles), -jnp.sin(angles)], axis=1).astype(jnp.bfloat16)

def rounded(values):
    return lax.optimization_barrier(values.astype(jnp.bfloat16)).astype(jnp.float32)

def one_frequency(operands):
    u_tiles, v_tiles, tile_ranks, spectrum, observed_f = operands
    u_full = u_tiles.astype(jnp.float32)
    v_full = v_tiles.astype(jnp.float32)
    rank_mask_array = (jnp.arange(RMAX, dtype=jnp.int32)[None, None, :] < tile_ranks[:, :, None]).astype(jnp.float32)[..., None]
    column_entries = spectrum.astype(jnp.float32).reshape(2, NV, NTC, TILE)
    swapped = jnp.stack([column_entries[1], -column_entries[0]])
    real_component = rounded(jnp.einsum('abckj,cvbj->abkv', v_full, column_entries) * rank_mask_array)
    imag_part = rounded(jnp.einsum('abckj,cvbj->abkv', v_full, swapped) * rank_mask_array)
    first_coef = jnp.stack([real_component, -imag_part], axis=2)
    second_coef = jnp.stack([imag_part, real_component], axis=2)
    predicted = jnp.stack([jnp.einsum('abcki,abckv->vai', u_full, first_coef), jnp.einsum('abcki,abckv->vai', u_full, second_coef)]).reshape(2, NV, NR)
    residual = observed_f - predicted
    row_data = rounded(residual).reshape(2, NV, NTR, TILE)
    swapped_rows = jnp.stack([row_data[1], -row_data[0]])
    real_component = rounded(jnp.einsum('abcki,cvai->abkv', u_full, row_data) * rank_mask_array)
    imag_part = rounded(jnp.einsum('abcki,cvai->abkv', u_full, swapped_rows) * rank_mask_array)
    first_coef = jnp.stack([real_component, -imag_part], axis=2)
    second_coef = jnp.stack([imag_part, real_component], axis=2)
    back_terms = jnp.stack([jnp.einsum('abckj,abckv->vbj', v_full, first_coef), jnp.einsum('abckj,abckv->vbj', v_full, second_coef)]).reshape(2, NV, NS)
    return (residual, back_terms.astype(jnp.bfloat16))

def reference(traces, u_bases, v_bases, ranks, observed):
    basis_lookup_table = dft_table(NF, FIRST_BIN, NT).astype(jnp.float32)
    flat_traces = traces.reshape(NV, NS, NT)

    def to_freq(trace_set):
        return jnp.einsum('kct,st->kcs', basis_lookup_table, trace_set.astype(jnp.float32)) * (1.0 / math.sqrt(NT))
    spectrum = lax.map(to_freq, flat_traces)
    spectrum = jnp.transpose(spectrum, (1, 2, 0, 3)).astype(jnp.bfloat16)
    residual, back_terms = lax.map(one_frequency, (u_bases, v_bases, ranks, spectrum, observed))
    back_full = back_terms.astype(jnp.float32)

    def to_time(index):
        spectra = back_full[:, :, index]
        return (jnp.einsum('kct,kcs->st', basis_lookup_table, spectra) * (1.0 / math.sqrt(NF))).astype(jnp.bfloat16)
    gradient = lax.map(to_time, jnp.arange(NV, dtype=jnp.int32)).reshape(NV, SBLK, SPOS, NT)
    return (residual, gradient)
```

```python
import math

import jax
import jax.numpy as jnp
from jax import lax
from jax.sharding import PartitionSpec as P

FIRST_BIN = 40


def dft_table(freq_count, first_bin, trace_len):
    freq_bins = first_bin + jnp.arange(freq_count, dtype=jnp.int32)
    time_steps = jnp.arange(trace_len, dtype=jnp.int32)
    phase_index = freq_bins[:, None] * time_steps[None, :] % trace_len
    angles = phase_index.astype(jnp.float32) * (2.0 * math.pi / trace_len)
    return jnp.stack([jnp.cos(angles), -jnp.sin(angles)], axis=1).astype(jnp.bfloat16)


def conj_project(basis_set, operand, einsum_form):
    swapped = jnp.stack([operand[:, 1], -operand[:, 0]], axis=1)
    real_component = jnp.einsum(einsum_form, basis_set, operand, preferred_element_type=jnp.float32)
    imag_part = jnp.einsum(einsum_form, basis_set, swapped, preferred_element_type=jnp.float32)
    return (real_component, imag_part)


def apply_ranks(real_component, imag_part, ranks, cap_used):
    rank_mask_array = (
        jnp.arange(cap_used, dtype=jnp.int32)[None, None, None, :] < ranks[..., None]
    ).astype(jnp.float32)[..., None]
    return (
        (real_component * rank_mask_array).astype(jnp.bfloat16),
        (imag_part * rank_mask_array).astype(jnp.bfloat16),
    )


def expand_terms(basis_set, real_component, imag_part, einsum_form):
    first_coef = jnp.stack([real_component, -imag_part], axis=3)
    second_coef = jnp.stack([imag_part, real_component], axis=3)
    return jnp.stack(
        [
            jnp.einsum(einsum_form, basis_set, first_coef, preferred_element_type=jnp.float32),
            jnp.einsum(einsum_form, basis_set, second_coef, preferred_element_type=jnp.float32),
        ],
        axis=1,
    )


def shards(traces, u_bases, v_bases, ranks, observed):
    local_freq = u_bases.shape[0]
    tiles_row = u_bases.shape[1]
    tiles_col = u_bases.shape[2]
    rank_cap = u_bases.shape[4]
    tile_len = u_bases.shape[5]
    virtual_source = observed.shape[2]
    freq_count = local_freq * lax.axis_size("freq")
    trace_len = traces.shape[3]
    basis_lookup_table = dft_table(freq_count, FIRST_BIN, trace_len)
    resident_traces = traces.reshape(traces.shape[0], traces.shape[2], trace_len)
    spectrum = (
        jnp.einsum(
            "gzq,odq->gzod", basis_lookup_table, resident_traces, preferred_element_type=jnp.float32
        )
        * (1.0 / math.sqrt(trace_len))
    ).astype(jnp.bfloat16)
    row_shards = lax.axis_size("trow")
    col_shards = lax.axis_size("tcol")
    spectrum = jnp.broadcast_to(spectrum[:, None], (freq_count, row_shards) + spectrum.shape[1:])
    spectrum = lax.all_to_all(
        spectrum.reshape((freq_count * row_shards,) + spectrum.shape[2:]),
        ("freq", "trow"),
        split_axis=0,
        concat_axis=0,
        tiled=True,
    )
    spectrum = spectrum.reshape((freq_count, row_shards) + spectrum.shape[1:])
    column_entries = spectrum.transpose(2, 0, 3, 1, 4).reshape(
        local_freq, 2, virtual_source, tiles_col, tile_len
    )
    real_component, imag_part = conj_project(v_bases, column_entries, "fabckj,fcvbj->fabkv")
    real_component, imag_part = apply_ranks(real_component, imag_part, ranks, rank_cap)
    row_terms = expand_terms(u_bases, real_component, imag_part, "fabcki,fabckv->fvai")
    row_terms = row_terms.reshape(local_freq, 2, virtual_source, tiles_row * tile_len)
    piece = tiles_row * tile_len // col_shards
    row_terms = row_terms.reshape(2 * virtual_source, col_shards, piece).transpose(1, 0, 2)
    row_terms = lax.all_to_all(
        row_terms.astype(jnp.bfloat16), "tcol", split_axis=0, concat_axis=0, tiled=True
    )
    row_piece = jnp.sum(row_terms.astype(jnp.float32), axis=0).astype(jnp.bfloat16)
    row_grand_total = lax.all_to_all(
        jnp.broadcast_to(row_piece[None], (col_shards,) + row_piece.shape),
        "tcol",
        split_axis=0,
        concat_axis=0,
        tiled=True,
    )
    row_grand_total = row_grand_total.transpose(1, 0, 2).reshape(observed.shape)
    row_grand_total = row_grand_total.astype(jnp.float32)
    residual = observed - row_grand_total
    row_data = residual.astype(jnp.bfloat16).reshape(
        local_freq, 2, virtual_source, tiles_row, tile_len
    )
    real_component, imag_part = conj_project(u_bases, row_data, "fabcki,fcvai->fabkv")
    real_component, imag_part = apply_ranks(real_component, imag_part, ranks, rank_cap)
    back_terms = expand_terms(v_bases, real_component, imag_part, "fabckj,fabckv->fvbj")
    back_terms = back_terms.reshape(2, freq_count, virtual_source // freq_count, tiles_col, tile_len)
    back_terms = back_terms.transpose(1, 3, 0, 2, 4).astype(jnp.bfloat16)
    back_terms = lax.all_to_all(
        back_terms.reshape((freq_count * row_shards,) + back_terms.shape[2:]),
        ("freq", "trow"),
        split_axis=0,
        concat_axis=0,
        tiled=True,
    )
    back_terms = back_terms.reshape((freq_count, row_shards) + back_terms.shape[1:])
    packed = jnp.sum(back_terms.astype(jnp.float32), axis=1).astype(jnp.bfloat16)
    values = jnp.einsum(
        "nuz,nuhr->hrz",
        basis_lookup_table,
        packed,
        preferred_element_type=jnp.float32,
    )
    result = (values * (1.0 / math.sqrt(freq_count))).astype(jnp.bfloat16)
    gradient = result.reshape(result.shape[0], 1, result.shape[1], trace_len)
    return (residual, gradient)


def solution(mesh):
    placed = (
        P("freq", "tcol", "trow", None),
        P("freq", "trow", "tcol", None, None, None),
        P("freq", "trow", "tcol", None, None, None),
        P("freq", "trow", "tcol"),
        P("freq", None, None, "trow"),
    )
    return jax.shard_map(
        shards,
        mesh=mesh,
        in_specs=placed,
        out_specs=(P("freq", None, None, "trow"), P("freq", "tcol", "trow", None)),
        check_vma=False,
    )
```

```python
import math

import jax
import jax.numpy as jnp
from jax import lax
from jax.experimental import pallas as pl
from jax.experimental.pallas import tpu as pltpu
from jax.sharding import PartitionSpec as P

FIRST_BIN = 40
LANES = 128
SUBLANES = 8
VMEM_LIMIT = 16 * 1024 * 1024


def dft_rows(freq_count, first_bin, trace_len):
    freq_bins = first_bin + jnp.arange(freq_count, dtype=jnp.int32)
    time_steps = jnp.arange(trace_len, dtype=jnp.int32)
    phase_index = freq_bins[:, None] * time_steps[None, :] % trace_len
    angles = phase_index.astype(jnp.float32) * (2.0 * math.pi / trace_len)
    return jnp.concatenate([jnp.cos(angles), -jnp.sin(angles)], axis=0).astype(jnp.bfloat16)


def contract_last(left, right):
    return lax.dot_general(
        left, right, (((1,), (1,)), ((), ())), preferred_element_type=jnp.float32
    )


def vmem_spec():
    return pl.BlockSpec(memory_space=pltpu.VMEM)


def any_spec():
    return pl.BlockSpec(memory_space=pl.ANY)


def params():
    return pltpu.CompilerParams(vmem_limit_bytes=VMEM_LIMIT)


def cost(flops, moved):
    return pl.CostEstimate(flops=flops, bytes_accessed=moved, transcendentals=0)


def spectrum_kernel(scale, copies_out, traces_ref, basis_ref, out_ref, held, rows, sems):
    sources, _, positions, _ = traces_ref.shape
    halves = positions // LANES
    freq_count = basis_ref.shape[0] // 2
    copies = []
    for g in range(sources):
        for h in range(halves):
            copy = pltpu.make_async_copy(
                traces_ref.at[g, 0, pl.ds(h * LANES, LANES)],
                held.at[g * halves + h],
                sems.at[g * halves + h],
            )
            copy.start()
            copies.append(copy)
    group = halves * 2 * sources
    for g in range(sources):
        for h in range(halves):
            copies[g * halves + h].wait()
            part = contract_last(basis_ref[...], held[g * halves + h]) * scale
            for c in range(2):
                rows[pl.ds((h * 2 + c) * sources + g, freq_count, stride=group), :] = part[
                    c * freq_count : (c + 1) * freq_count
                ]
    for f in range(freq_count):
        piece = rows[f * group : (f + 1) * group, :].astype(jnp.bfloat16)
        for r in range(copies_out):
            out_ref[f * copies_out + r] = piece


def combined(top, bottom, mask):
    lane = lax.broadcasted_iota(jnp.int32, top.shape, 1)
    first = (lane // 32) % 2 == 0

    def swapped(x):
        return jnp.where(
            first, -pltpu.roll(x, LANES - 32, 1), pltpu.roll(x, 32, 1)
        )

    new_top = (top - swapped(bottom)) * mask
    new_bottom = (bottom + swapped(top)) * mask
    return new_top.astype(jnp.bfloat16), new_bottom.astype(jnp.bfloat16)


def forward_kernel(spec_ref, v_ref, u_ref, mask_ref, out_ref, rows, held):
    chunks, group, _ = spec_ref.shape
    tiles_row, tiles_col = v_ref.shape[1:3]
    owners = chunks // tiles_col
    sources = group // 4
    virtual = owners * sources
    for n in range(chunks):
        rows[n * group : (n + 1) * group, :] = spec_ref[n].astype(jnp.float32)
    for b in range(tiles_col):
        for h in range(2):
            pieces = [
                rows[pl.ds(b * group + h * 2 * sources + i, owners, stride=tiles_col * group), :]
                for i in range(2 * sources)
            ]
            held[b * 2 * virtual : (b + 1) * 2 * virtual, h * LANES : (h + 1) * LANES] = (
                jnp.concatenate(pieces, axis=0).astype(jnp.bfloat16)
            )
    width = tiles_col * 64
    spectra = held[...]
    per_half = LANES // 64
    for a in range(tiles_row):
        bases = v_ref[0, a].reshape(width, v_ref.shape[5])
        products = contract_last(spectra, bases)
        tops, bottoms = [], []
        for h in range(width // LANES):
            lanes = slice(h * LANES, (h + 1) * LANES)
            lane = lax.broadcasted_iota(jnp.int32, (2 * virtual, LANES), 1)
            low = products[(2 * h) * 2 * virtual : (2 * h + 1) * 2 * virtual, lanes]
            high = products[(2 * h + 1) * 2 * virtual : (2 * h + 2) * 2 * virtual, lanes]
            chosen = jnp.where(lane < 64, low, high)
            top, bottom = combined(chosen[:virtual], chosen[virtual:], mask_ref[a : a + 1, lanes])
            tops.append(top)
            bottoms.append(bottom)
        left = jnp.concatenate(
            [jnp.concatenate(tops, axis=1), jnp.concatenate(bottoms, axis=1)], axis=0
        )
        terms = jnp.dot(
            left, u_ref[0, a].reshape(width, u_ref.shape[5]), preferred_element_type=jnp.float32
        ).astype(jnp.bfloat16)
        for h in range(2):
            out_ref[2 * a + h] = terms[:, h * LANES : (h + 1) * LANES]


def sum_kernel(sources, parts_ref, out_ref, rows):
    count, height, _ = parts_ref.shape
    total = parts_ref[0].astype(jnp.float32)
    for n in range(1, count):
        total = total + parts_ref[n].astype(jnp.float32)
    virtual = height // 2
    owners = virtual // sources
    for c in range(2):
        for g in range(sources):
            start = c * virtual + g * owners
            rows[pl.ds(c * virtual + g, owners, stride=sources), :] = total[start : start + owners]
    piece = rows[...].astype(jnp.bfloat16)
    for n in range(count):
        out_ref[n] = piece


def adjoint_kernel(
    sources, observed_ref, total_ref, u_ref, v_ref, mask_ref, residual_ref, out_ref, rows, ordered
):
    chunks, group, _ = out_ref.shape
    tiles_row, tiles_col = u_ref.shape[1:3]
    virtual = observed_ref.shape[2]
    owners = chunks // tiles_col
    width = tiles_col * 64
    total = None
    lane = lax.broadcasted_iota(jnp.int32, (2 * virtual, LANES), 1)
    nothing = jnp.zeros((2 * virtual, LANES), jnp.bfloat16)
    for a in range(tiles_row):
        data = []
        for h in range(2):
            n = 2 * a + h
            lanes = slice(n * LANES, (n + 1) * LANES)
            predicted = total_ref[n].astype(jnp.float32)
            parts = []
            for c in range(2):
                left = observed_ref[0, c, :, lanes] - predicted[c * virtual : (c + 1) * virtual]
                residual_ref[0, c, :, lanes] = left
                parts.append(left.astype(jnp.bfloat16))
            data.append(jnp.concatenate(parts, axis=0))
        products = contract_last(
            jnp.concatenate(data, axis=1), u_ref[0, a].reshape(width, u_ref.shape[5])
        )
        blocks = []
        for h in range(width // LANES):
            lanes = slice(h * LANES, (h + 1) * LANES)
            top, bottom = combined(
                products[:virtual, lanes], products[virtual:, lanes], mask_ref[a : a + 1, lanes]
            )
            both = jnp.concatenate([top, bottom], axis=0)
            for low in (True, False):
                chosen = jnp.where((lane < 64) == low, both, nothing)
                blocks.append(
                    jnp.concatenate([chosen if h == k else nothing for k in range(width // LANES)], axis=1)
                )
        terms = jnp.dot(
            jnp.concatenate(blocks, axis=0),
            v_ref[0, a].reshape(width, v_ref.shape[5]),
            preferred_element_type=jnp.float32,
        )
        total = terms if total is None else total + terms
    for h in range(2):
        rows[h] = total[:, h * LANES : (h + 1) * LANES]
    for b in range(tiles_col):
        for h in range(2):
            for c in range(2):
                for g in range(sources):
                    ordered[
                        pl.ds(
                            b * group + (h * 2 + c) * sources + g, owners, stride=tiles_col * group
                        ),
                        :,
                    ] = rows[h, pl.ds((b * 2 + c) * virtual + g, owners, stride=sources), :]
    for n in range(chunks):
        out_ref[n] = ordered[n * group : (n + 1) * group, :].astype(jnp.bfloat16)


def back_kernel(scale, copies_in, parts_ref, basis_ref, out_ref, rows):
    chunks, group, _ = parts_ref.shape
    freq_count = chunks // copies_in
    sources = group // 4
    for f in range(freq_count):
        total = parts_ref[f * copies_in].astype(jnp.float32)
        for r in range(1, copies_in):
            total = total + parts_ref[f * copies_in + r].astype(jnp.float32)
        rows[f * group : (f + 1) * group, :] = total
    basis = basis_ref[...]
    for g in range(sources):
        for h in range(2):
            spectra = jnp.concatenate(
                [
                    rows[pl.ds((h * 2 + c) * sources + g, freq_count, stride=group), :]
                    for c in range(2)
                ],
                axis=0,
            ).astype(jnp.bfloat16)
            values = lax.dot_general(
                spectra, basis, (((0,), (0,)), ((), ())), preferred_element_type=jnp.float32
            )
            out_ref[g, 0, h * LANES : (h + 1) * LANES, :] = (values * scale).astype(jnp.bfloat16)


def spectrum_chunks(traces, basis, row_shards):
    sources, _, positions, trace_len = traces.shape
    freq_count = basis.shape[0] // 2
    halves = positions // LANES
    group = halves * 2 * sources
    return pl.pallas_call(
        lambda *refs: spectrum_kernel(1.0 / math.sqrt(trace_len), row_shards, *refs),
        out_shape=jax.ShapeDtypeStruct((freq_count * row_shards, group, LANES), jnp.bfloat16),
        in_specs=[any_spec(), vmem_spec()],
        out_specs=vmem_spec(),
        scratch_shapes=[
            pltpu.VMEM((sources * halves, LANES, trace_len), jnp.bfloat16),
            pltpu.VMEM((freq_count * group, LANES), jnp.float32),
            pltpu.SemaphoreType.DMA((sources * halves,)),
        ],
        compiler_params=params(),
        cost_estimate=cost(2 * 2 * freq_count * traces.size, 2 * traces.size),
        name="spectrum",
    )(traces, basis)


def forward_chunks(spectra, v_bases, u_bases, mask, virtual):
    tiles_row, tiles_col = u_bases.shape[1:3]
    tile_len = u_bases.shape[5]
    return pl.pallas_call(
        forward_kernel,
        out_shape=jax.ShapeDtypeStruct((2 * tiles_row, 2 * virtual, LANES), jnp.bfloat16),
        in_specs=[vmem_spec()] * 4,
        out_specs=vmem_spec(),
        scratch_shapes=[
            pltpu.VMEM((spectra.shape[0] * spectra.shape[1], LANES), jnp.float32),
            pltpu.VMEM((tiles_col * 2 * virtual, tile_len), jnp.bfloat16),
        ],
        compiler_params=params(),
        cost_estimate=cost(8 * virtual * u_bases.size, 4 * u_bases.size),
        name="forward",
    )(spectra, v_bases, u_bases, mask)


def summed_chunks(parts, sources):
    return pl.pallas_call(
        lambda *refs: sum_kernel(sources, *refs),
        out_shape=jax.ShapeDtypeStruct(parts.shape, jnp.bfloat16),
        in_specs=[vmem_spec()],
        out_specs=vmem_spec(),
        scratch_shapes=[pltpu.VMEM(parts.shape[1:], jnp.float32)],
        compiler_params=params(),
        cost_estimate=cost(parts.size, 4 * parts.size),
        name="total",
    )(parts)


def adjoint_chunks(observed, total, u_bases, v_bases, mask, sources):
    tiles_col = u_bases.shape[2]
    tile_len = u_bases.shape[5]
    virtual = observed.shape[2]
    group = 4 * sources
    chunks = tiles_col * virtual // sources
    return pl.pallas_call(
        lambda *refs: adjoint_kernel(sources, *refs),
        out_shape=(
            jax.ShapeDtypeStruct(observed.shape, jnp.float32),
            jax.ShapeDtypeStruct((chunks, group, LANES), jnp.bfloat16),
        ),
        in_specs=[vmem_spec()] * 5,
        out_specs=(vmem_spec(), vmem_spec()),
        scratch_shapes=[
            pltpu.VMEM((tile_len // LANES, tiles_col * 2 * virtual, LANES), jnp.float32),
            pltpu.VMEM((chunks * group, LANES), jnp.float32),
        ],
        compiler_params=params(),
        cost_estimate=cost(8 * virtual * u_bases.size, 4 * u_bases.size),
        name="adjoint",
    )(observed, total, u_bases, v_bases, mask)


def back_traces(parts, basis, row_shards, shape):
    freq_count = basis.shape[0] // 2
    group = parts.shape[1]
    return pl.pallas_call(
        lambda *refs: back_kernel(1.0 / math.sqrt(freq_count), row_shards, *refs),
        out_shape=jax.ShapeDtypeStruct(shape, jnp.bfloat16),
        in_specs=[vmem_spec(), vmem_spec()],
        out_specs=vmem_spec(),
        scratch_shapes=[pltpu.VMEM((freq_count * group, LANES), jnp.float32)],
        compiler_params=params(),
        cost_estimate=cost(4 * freq_count * math.prod(shape), 2 * math.prod(shape)),
        name="back",
    )(parts, basis)


def shards(traces, u_bases, v_bases, ranks, observed):
    tiles_row, tiles_col = u_bases.shape[1:3]
    rank_cap = u_bases.shape[4]
    virtual = observed.shape[2]
    sources = traces.shape[0]
    freq_count = u_bases.shape[0] * lax.axis_size("freq")
    row_shards = lax.axis_size("trow")
    basis = dft_rows(freq_count, FIRST_BIN, traces.shape[3])
    mask = jnp.arange(rank_cap, dtype=jnp.int32) < ranks[0, :, :, None, None]
    mask = jnp.broadcast_to(mask, (tiles_row, tiles_col, 2, rank_cap))
    mask = mask.astype(jnp.float32).reshape(tiles_row, tiles_col * 2 * rank_cap)

    def exchange(chunks, axes):
        return lax.all_to_all(chunks, axes, split_axis=0, concat_axis=0, tiled=True)

    spectra = exchange(spectrum_chunks(traces, basis, row_shards), ("freq", "trow"))
    terms = exchange(forward_chunks(spectra, v_bases, u_bases, mask, virtual), "tcol")
    total = exchange(summed_chunks(terms, sources), "tcol")
    residual, back = adjoint_chunks(observed, total, u_bases, v_bases, mask, sources)
    back = exchange(back, ("freq", "trow"))
    return residual, back_traces(back, basis, row_shards, traces.shape)


def solution(mesh):
    placed = (
        P("freq", "tcol", "trow", None),
        P("freq", "trow", "tcol", None, None, None),
        P("freq", "trow", "tcol", None, None, None),
        P("freq", "trow", "tcol"),
        P("freq", None, None, "trow"),
    )
    return jax.shard_map(
        shards,
        mesh=mesh,
        in_specs=placed,
        out_specs=(P("freq", None, None, "trow"), P("freq", "tcol", "trow", None)),
        check_vma=False,
    )
```

```python
import math

import jax
import jax.numpy as jnp
from jax import lax
from jax.experimental import pallas as pl
from jax.experimental.pallas import tpu as pltpu
from jax.sharding import PartitionSpec as P

FIRST_BIN = 40
LANES = 128
SUBLANES = 8
VMEM_LIMIT = 16 * 1024 * 1024
VMEM_MOST = 60 * 1024 * 1024
VMEM_FETCH = 16 * 1024 * 1024


def dft_angles(freq_bins, time_steps, trace_len):
    phase_index = freq_bins * time_steps % trace_len
    return phase_index.astype(jnp.float32) * (2.0 * math.pi / trace_len)


def contract_last(left, right):
    return lax.dot_general(
        left, right, (((1,), (1,)), ((), ())), preferred_element_type=jnp.float32
    )


def vmem_spec():
    return pl.BlockSpec(memory_space=pltpu.VMEM)


def hbm_spec():
    return pl.BlockSpec(memory_space=pltpu.HBM)


def params(limit=VMEM_LIMIT):
    return pltpu.CompilerParams(vmem_limit_bytes=limit)


def cost(flops, moved):
    return pl.CostEstimate(flops=flops, bytes_accessed=moved, transcendentals=0)


def spectrum_kernel(scale, copies_out, traces_ref, out_ref, basis_ref, held, rows, sems):
    sources, _, positions, trace_len = traces_ref.shape
    halves = positions // LANES
    freq_count = basis_ref.shape[0] // 2
    copies = []
    for g in range(sources):
        for h in range(halves):
            copy = pltpu.make_async_copy(
                traces_ref.at[g, 0, pl.ds(h * LANES, LANES)],
                held.at[g * halves + h],
                sems.at[g * halves + h],
            )
            copy.start()
            copies.append(copy)
    row = lax.broadcasted_iota(jnp.int32, basis_ref.shape, 0)
    time = lax.broadcasted_iota(jnp.int32, basis_ref.shape, 1)
    angles = dft_angles(FIRST_BIN + row % freq_count, time, trace_len)
    basis_ref[...] = jnp.where(row < freq_count, jnp.cos(angles), -jnp.sin(angles)).astype(
        jnp.bfloat16
    )
    group = halves * 2 * sources
    for g in range(sources):
        for h in range(halves):
            copies[g * halves + h].wait()
    basis = basis_ref[...]
    part = contract_last(basis, held[...].reshape(sources * halves * LANES, trace_len)) * scale
    for g in range(sources):
        for h in range(halves):
            for c in range(2):
                rows[pl.ds((h * 2 + c) * sources + g, freq_count, stride=group), :] = part[
                    c * freq_count : (c + 1) * freq_count, (g * halves + h) * LANES : (g * halves + h + 1) * LANES
                ]
    for f in range(freq_count):
        piece = rows[f * group : (f + 1) * group, :].astype(jnp.bfloat16)
        for r in range(copies_out):
            out_ref[f * copies_out + r] = piece


def fetch_kernel(
    u_hbm, v_hbm, ranks_hbm, after, u_ref, v_ref, by_row_ref, by_col_ref, ranks_ref, sems
):
    del after
    tiles_row, tiles_col, _, rank_cap, _ = u_ref.shape[1:]
    rank_copy = pltpu.make_async_copy(ranks_hbm, ranks_ref, sems.at[0])
    v_copy = pltpu.make_async_copy(v_hbm, v_ref, sems.at[1])
    u_copy = pltpu.make_async_copy(u_hbm, u_ref, sems.at[2])
    rank_copy.start()
    v_copy.start()
    u_copy.start()
    rank_copy.wait()
    lane = lax.broadcasted_iota(jnp.int32, (1, LANES), 1)
    rank = lane % rank_cap
    low = lane < 2 * rank_cap
    for a in range(tiles_row):
        for b in range(0, tiles_col, 2):
            cap = jnp.where(low, ranks_ref[b, a], ranks_ref[b + 1, a])
            lanes = slice(b * 2 * rank_cap, (b + 2) * 2 * rank_cap)
            by_row_ref[a : a + 1, lanes] = jnp.where(rank < cap, 1.0, 0.0)
    for b in range(tiles_col):
        for a in range(0, tiles_row, 2):
            cap = jnp.where(low, ranks_ref[b, a], ranks_ref[b, a + 1])
            lanes = slice(a * 2 * rank_cap, (a + 2) * 2 * rank_cap)
            by_col_ref[b : b + 1, lanes] = jnp.where(rank < cap, 1.0, 0.0)
    v_copy.wait()
    u_copy.wait()


def combined(top, bottom, mask):
    lane = lax.broadcasted_iota(jnp.int32, top.shape, 1)
    first = (lane // 32) % 2 == 0

    def swapped(x):
        return jnp.where(
            first, -pltpu.roll(x, LANES - 32, 1), pltpu.roll(x, 32, 1)
        )

    new_top = (top - swapped(bottom)) * mask
    new_bottom = (bottom + swapped(top)) * mask
    return jnp.concatenate([new_top, new_bottom], axis=0).astype(jnp.bfloat16)


def forward_kernel(spec_ref, v_ref, u_ref, mask_ref, out_ref, rows):
    chunks, group, _ = spec_ref.shape
    tiles_row, tiles_col, _, rank_cap, tile_len = v_ref.shape[1:]
    owners = chunks // tiles_col
    sources = group // 4
    virtual = owners * sources
    for n in range(chunks):
        rows[n * group : (n + 1) * group, :] = spec_ref[n].astype(jnp.float32)
    products = []
    for b in range(tiles_col):
        spectra = jnp.concatenate(
            [
                jnp.concatenate(
                    [
                        rows[
                            pl.ds(b * group + h * 2 * sources + i, owners, stride=tiles_col * group),
                            :,
                        ]
                        for i in range(2 * sources)
                    ],
                    axis=0,
                )
                for h in range(2)
            ],
            axis=1,
        ).astype(jnp.bfloat16)
        bases = v_ref[0, :, b].reshape(tiles_row * 2 * rank_cap, tile_len)
        products.append(contract_last(spectra, bases))
    lane = lax.broadcasted_iota(jnp.int32, (2 * virtual, LANES), 1)
    nothing = jnp.zeros((2 * virtual, LANES), jnp.bfloat16)
    for p in range(tiles_row // 2):
        lanes = slice(p * LANES, (p + 1) * LANES)
        evens, odds = [], []
        for b in range(tiles_col):
            both = combined(
                products[b][:virtual, lanes],
                products[b][virtual:, lanes],
                mask_ref[b : b + 1, lanes],
            )
            evens.append(jnp.where(lane < 64, both, nothing))
            odds.append(jnp.where(lane < 64, nothing, both))
        left = jnp.concatenate(
            [jnp.concatenate(evens, axis=1), jnp.concatenate(odds, axis=1)], axis=0
        )
        bases = jnp.concatenate(
            [
                u_ref[0, 2 * p + i, b].reshape(2 * rank_cap, tile_len)
                for b in range(tiles_col)
                for i in range(2)
            ],
            axis=0,
        )
        terms = jnp.dot(left, bases, preferred_element_type=jnp.float32).astype(jnp.bfloat16)
        for i in range(2):
            for h in range(2):
                out_ref[2 * (2 * p + i) + h] = terms[
                    i * 2 * virtual : (i + 1) * 2 * virtual, h * LANES : (h + 1) * LANES
                ]


def sum_kernel(sources, parts_ref, out_ref, rows):
    count, height, _ = parts_ref.shape
    total = parts_ref[0].astype(jnp.float32)
    for n in range(1, count):
        total = total + parts_ref[n].astype(jnp.float32)
    virtual = height // 2
    owners = virtual // sources
    for c in range(2):
        for g in range(sources):
            start = c * virtual + g * owners
            rows[pl.ds(c * virtual + g, owners, stride=sources), :] = total[start : start + owners]
    piece = rows[...].astype(jnp.bfloat16)
    for n in range(count):
        out_ref[n] = piece


def adjoint_kernel(
    sources,
    observed_ref,
    total_ref,
    u_ref,
    v_ref,
    mask_ref,
    residual_ref,
    out_ref,
    rows,
    ordered,
    sems,
):
    chunks, group, _ = out_ref.shape
    tiles_row, tiles_col, _, rank_cap, tile_len = u_ref.shape[1:]
    virtual = observed_ref.shape[2]
    owners = chunks // tiles_col
    width = tiles_col * 2 * rank_cap
    pairs = width // LANES
    lane = lax.broadcasted_iota(jnp.int32, (2 * virtual, LANES), 1)
    nothing = jnp.zeros((2 * virtual, LANES), jnp.bfloat16)
    firsts = [[] for _ in range(pairs)]
    seconds = [[] for _ in range(pairs)]
    copies = []
    for a in range(tiles_row):
        data = []
        for h in range(2):
            n = 2 * a + h
            lanes = slice(n * LANES, (n + 1) * LANES)
            predicted = total_ref[n].astype(jnp.float32)
            parts = []
            for c in range(2):
                left = observed_ref[0, c, :, lanes] - predicted[c * virtual : (c + 1) * virtual]
                residual_ref[0, c, :, lanes] = left
                parts.append(left.astype(jnp.bfloat16))
            data.append(jnp.concatenate(parts, axis=0))
        products = contract_last(
            jnp.concatenate(data, axis=1), u_ref[0, a].reshape(width, tile_len)
        )
        for h in range(pairs):
            lanes = slice(h * LANES, (h + 1) * LANES)
            both = combined(
                products[:virtual, lanes], products[virtual:, lanes], mask_ref[a : a + 1, lanes]
            )
            firsts[h].append(jnp.where(lane < 64, both, nothing))
            seconds[h].append(jnp.where(lane < 64, nothing, both))
    for h in range(pairs):
        left = jnp.concatenate(
            [jnp.concatenate(firsts[h], axis=1), jnp.concatenate(seconds[h], axis=1)], axis=0
        )
        bases = v_ref[0, :, 2 * h : 2 * h + 2].reshape(tiles_row * LANES, tile_len)
        terms = jnp.dot(left, bases, preferred_element_type=jnp.float32)
        for k in range(2):
            rows[k, h * 4 * virtual : (h + 1) * 4 * virtual, :] = terms[:, k * LANES : (k + 1) * LANES]
    for b in range(tiles_col):
        for h in range(2):
            for c in range(2):
                for g in range(sources):
                    ordered[
                        pl.ds(
                            b * group + (h * 2 + c) * sources + g, owners, stride=tiles_col * group
                        ),
                        :,
                    ] = rows[h, pl.ds((b * 2 + c) * virtual + g, owners, stride=sources), :]
    for n in range(chunks):
        out_ref[n] = ordered[n * group : (n + 1) * group, :].astype(jnp.bfloat16)
    for copy in copies:
        copy.wait()


def back_kernel(
    scale, copies_in, residual_ref, parts_ref, basis_ref, residual_hbm, out_hbm, rows, held, sems
):
    pieces = held.shape[0]
    kept = pltpu.make_async_copy(residual_ref, residual_hbm, sems.at[pieces])
    kept.start()
    chunks, group, _ = parts_ref.shape
    freq_count = chunks // copies_in
    sources = group // 4
    for f in range(freq_count):
        total = parts_ref[f * copies_in].astype(jnp.float32)
        for r in range(1, copies_in):
            total = total + parts_ref[f * copies_in + r].astype(jnp.float32)
        rows[f * group : (f + 1) * group, :] = total
    basis = basis_ref[...]
    copies = [kept]
    for g in range(sources):
        for h in range(2):
            spectra = jnp.concatenate(
                [
                    rows[pl.ds((h * 2 + c) * sources + g, freq_count, stride=group), :]
                    for c in range(2)
                ],
                axis=0,
            ).astype(jnp.bfloat16)
            values = lax.dot_general(
                spectra, basis, (((0,), (0,)), ((), ())), preferred_element_type=jnp.float32
            )
            held[g * 2 + h] = (values * scale).astype(jnp.bfloat16)
            copy = pltpu.make_async_copy(
                held.at[g * 2 + h],
                out_hbm.at[g, 0, pl.ds(h * LANES, LANES)],
                sems.at[g * 2 + h],
            )
            copy.start()
            copies.append(copy)
    for copy in copies:
        copy.wait()


def spectrum_chunks(traces, freq_count, row_shards):
    sources, _, positions, trace_len = traces.shape
    halves = positions // LANES
    group = halves * 2 * sources
    return pl.pallas_call(
        lambda *refs: spectrum_kernel(1.0 / math.sqrt(trace_len), row_shards, *refs),
        out_shape=(
            jax.ShapeDtypeStruct((freq_count * row_shards, group, LANES), jnp.bfloat16),
            jax.ShapeDtypeStruct((2 * freq_count, trace_len), jnp.bfloat16),
        ),
        in_specs=[hbm_spec()],
        out_specs=(vmem_spec(), vmem_spec()),
        scratch_shapes=[
            pltpu.VMEM((sources * halves, LANES, trace_len), jnp.bfloat16),
            pltpu.VMEM((freq_count * group, LANES), jnp.float32),
            pltpu.SemaphoreType.DMA((sources * halves,)),
        ],
        compiler_params=params(VMEM_MOST),
        cost_estimate=cost(2 * 2 * freq_count * traces.size, 2 * traces.size),
        name="spectrum",
    )(traces)


def fetched(u_bases, v_bases, ranks, after):
    tiles_row, tiles_col, _, rank_cap, _ = u_bases.shape[1:]
    return pl.pallas_call(
        fetch_kernel,
        out_shape=(
            jax.ShapeDtypeStruct(u_bases.shape, jnp.bfloat16),
            jax.ShapeDtypeStruct(v_bases.shape, jnp.bfloat16),
            jax.ShapeDtypeStruct((tiles_row, tiles_col * 2 * rank_cap), jnp.float32),
            jax.ShapeDtypeStruct((tiles_col, tiles_row * 2 * rank_cap), jnp.float32),
        ),
        in_specs=[hbm_spec()] * 4,
        out_specs=(vmem_spec(),) * 4,
        scratch_shapes=[
            pltpu.SMEM((tiles_col, tiles_row), jnp.int32),
            pltpu.SemaphoreType.DMA((3,)),
        ],
        compiler_params=params(VMEM_FETCH),
        cost_estimate=cost(0, 4 * u_bases.size),
        name="fetch",
    )(u_bases, v_bases, ranks, after)


def forward_chunks(spectra, v_bases, u_bases, mask, virtual):
    tiles_row = u_bases.shape[1]
    return pl.pallas_call(
        forward_kernel,
        out_shape=jax.ShapeDtypeStruct((2 * tiles_row, 2 * virtual, LANES), jnp.bfloat16),
        in_specs=[vmem_spec()] * 4,
        out_specs=vmem_spec(),
        scratch_shapes=[
            pltpu.VMEM((spectra.shape[0] * spectra.shape[1], LANES), jnp.float32),
        ],
        compiler_params=params(),
        cost_estimate=cost(8 * virtual * u_bases.size, 4 * u_bases.size),
        name="forward",
    )(spectra, v_bases, u_bases, mask)


def summed_chunks(parts, sources):
    return pl.pallas_call(
        lambda *refs: sum_kernel(sources, *refs),
        out_shape=jax.ShapeDtypeStruct(parts.shape, jnp.bfloat16),
        in_specs=[vmem_spec()],
        out_specs=vmem_spec(),
        scratch_shapes=[pltpu.VMEM(parts.shape[1:], jnp.float32)],
        compiler_params=params(),
        cost_estimate=cost(parts.size, 4 * parts.size),
        name="total",
    )(parts)


def adjoint_chunks(observed, total, u_bases, v_bases, mask, sources):
    tiles_col = u_bases.shape[2]
    tile_len = u_bases.shape[5]
    virtual = observed.shape[2]
    group = 4 * sources
    chunks = tiles_col * virtual // sources
    return pl.pallas_call(
        lambda *refs: adjoint_kernel(sources, *refs),
        out_shape=(
            jax.ShapeDtypeStruct(observed.shape, jnp.float32),
            jax.ShapeDtypeStruct((chunks, group, LANES), jnp.bfloat16),
        ),
        in_specs=[vmem_spec()] * 5,
        out_specs=(vmem_spec(), vmem_spec()),
        scratch_shapes=[
            pltpu.VMEM((tile_len // LANES, tiles_col * 2 * virtual, LANES), jnp.float32),
            pltpu.VMEM((chunks * group, LANES), jnp.float32),
            pltpu.SemaphoreType.DMA((u_bases.shape[1] // 4,)),
        ],
        compiler_params=params(),
        cost_estimate=cost(8 * virtual * u_bases.size, 4 * u_bases.size),
        name="adjoint",
    )(observed, total, u_bases, v_bases, mask)


def back_traces(residual, parts, basis, row_shards, shape):
    freq_count = basis.shape[0] // 2
    group = parts.shape[1]
    pieces = shape[0] * shape[2] // LANES
    return pl.pallas_call(
        lambda *refs: back_kernel(1.0 / math.sqrt(freq_count), row_shards, *refs),
        out_shape=(
            jax.ShapeDtypeStruct(residual.shape, jnp.float32),
            jax.ShapeDtypeStruct(shape, jnp.bfloat16),
        ),
        in_specs=[vmem_spec()] * 3,
        out_specs=(hbm_spec(), hbm_spec()),
        scratch_shapes=[
            pltpu.VMEM((freq_count * group, LANES), jnp.float32),
            pltpu.VMEM((pieces, LANES, shape[3]), jnp.bfloat16),
            pltpu.SemaphoreType.DMA((pieces + 1,)),
        ],
        compiler_params=params(),
        cost_estimate=cost(4 * freq_count * math.prod(shape), 2 * math.prod(shape)),
        name="back",
    )(residual, parts, basis)


def shards(traces, u_bases, v_bases, ranks, observed):
    virtual = observed.shape[2]
    sources = traces.shape[0]
    freq_count = u_bases.shape[0] * lax.axis_size("freq")
    row_shards = lax.axis_size("trow")

    def exchange(chunks, axes):
        return lax.all_to_all(chunks, axes, split_axis=0, concat_axis=0, tiled=True)

    spectra, basis = spectrum_chunks(traces, freq_count, row_shards)
    u_held, v_held, by_row, by_col = fetched(u_bases, v_bases, ranks[0].T, spectra)
    spectra = exchange(spectra, ("freq", "trow"))
    terms = exchange(forward_chunks(spectra, v_held, u_held, by_col, virtual), "tcol")
    total = exchange(summed_chunks(terms, sources), "tcol")
    residual, back = adjoint_chunks(observed, total, u_held, v_held, by_row, sources)
    back = exchange(back, ("freq", "trow"))
    return back_traces(residual, back, basis, row_shards, traces.shape)


def solution(mesh):
    placed = (
        P("freq", "tcol", "trow", None),
        P("freq", "trow", "tcol", None, None, None),
        P("freq", "trow", "tcol", None, None, None),
        P("freq", "trow", "tcol"),
        P("freq", None, None, "trow"),
    )
    return jax.shard_map(
        shards,
        mesh=mesh,
        in_specs=placed,
        out_specs=(P("freq", None, None, "trow"), P("freq", "tcol", "trow", None)),
        check_vma=False,
    )
```

```python
import math

import jax
import jax.numpy as jnp
from jax import lax
from jax.experimental import pallas as pl
from jax.experimental.pallas import tpu as pltpu
from jax.sharding import PartitionSpec as P

FIRST_BIN = 40
LANES = 128
SUBLANES = 8
VMEM_LIMIT = 16 * 1024 * 1024


def dft_angles(freq_bins, time_steps, trace_len):
    phase_index = freq_bins * time_steps % trace_len
    return phase_index.astype(jnp.float32) * (2.0 * math.pi / trace_len)


def contract_last(left, right):
    return lax.dot_general(
        left, right, (((1,), (1,)), ((), ())), preferred_element_type=jnp.float32
    )


def vmem_spec():
    return pl.BlockSpec(memory_space=pltpu.VMEM)


def hbm_spec():
    return pl.BlockSpec(memory_space=pltpu.HBM)


def in_hbm(array):
    return pltpu.with_memory_space_constraint(array, pltpu.HBM)


def params():
    return pltpu.CompilerParams(vmem_limit_bytes=VMEM_LIMIT)


def cost(flops, moved):
    return pl.CostEstimate(flops=flops, bytes_accessed=moved, transcendentals=0)


def spectrum_kernel(
    scale,
    copies_out,
    traces_hbm,
    u_hbm,
    v_hbm,
    ranks_hbm,
    out_ref,
    basis_ref,
    u_ref,
    v_ref,
    by_row_ref,
    by_col_ref,
    held,
    rows,
    ranks_ref,
    sems,
):
    sources, _, positions, trace_len = traces_hbm.shape
    halves = positions // LANES
    freq_count = basis_ref.shape[0] // 2
    tiles_row, tiles_col, _, rank_cap, _ = u_ref.shape[1:]
    rank_copy = pltpu.make_async_copy(ranks_hbm, ranks_ref, sems.at[0])
    v_copy = pltpu.make_async_copy(v_hbm, v_ref, sems.at[1])
    u_copy = pltpu.make_async_copy(u_hbm, u_ref, sems.at[2])
    copies = []
    for g in range(sources):
        for h in range(halves):
            copies.append(
                pltpu.make_async_copy(
                    traces_hbm.at[g, 0, pl.ds(h * LANES, LANES)],
                    held.at[g * halves + h],
                    sems.at[3 + g * halves + h],
                )
            )
    for copy in copies:
        copy.start()
    rank_copy.start()
    v_copy.start()
    u_copy.start()

    row = lax.broadcasted_iota(jnp.int32, basis_ref.shape, 0)
    time = lax.broadcasted_iota(jnp.int32, basis_ref.shape, 1)
    angles = dft_angles(FIRST_BIN + row % freq_count, time, trace_len)
    basis_ref[...] = jnp.where(row < freq_count, jnp.cos(angles), -jnp.sin(angles)).astype(
        jnp.bfloat16
    )
    rank_copy.wait()
    lane = lax.broadcasted_iota(jnp.int32, (1, LANES), 1)
    rank = lane % rank_cap
    low = lane < 2 * rank_cap
    for a in range(tiles_row):
        for b in range(0, tiles_col, 2):
            cap = jnp.where(low, ranks_ref[b, a], ranks_ref[b + 1, a])
            lanes = slice(b * 2 * rank_cap, (b + 2) * 2 * rank_cap)
            by_row_ref[a : a + 1, lanes] = jnp.where(rank < cap, 1.0, 0.0)
    for b in range(tiles_col):
        for a in range(0, tiles_row, 2):
            cap = jnp.where(low, ranks_ref[b, a], ranks_ref[b, a + 1])
            lanes = slice(a * 2 * rank_cap, (a + 2) * 2 * rank_cap)
            by_col_ref[b : b + 1, lanes] = jnp.where(rank < cap, 1.0, 0.0)

    group = halves * 2 * sources
    for copy in copies:
        copy.wait()
    spectra = (
        contract_last(basis_ref[...], held[...].reshape(sources * halves * LANES, trace_len))
        * scale
    )
    for g in range(sources):
        for h in range(halves):
            lanes = slice((g * halves + h) * LANES, (g * halves + h + 1) * LANES)
            for c in range(2):
                rows[pl.ds((h * 2 + c) * sources + g, freq_count, stride=group), :] = spectra[
                    c * freq_count : (c + 1) * freq_count, lanes
                ]
    for f in range(freq_count):
        piece = rows[f * group : (f + 1) * group, :].astype(jnp.bfloat16)
        for r in range(copies_out):
            out_ref[f * copies_out + r] = piece
    v_copy.wait()
    u_copy.wait()


def combined(top, bottom, mask):
    lane = lax.broadcasted_iota(jnp.int32, top.shape, 1)
    first = (lane // 32) % 2 == 0

    def swapped(x):
        return jnp.where(
            first, -pltpu.roll(x, LANES - 32, 1), pltpu.roll(x, 32, 1)
        )

    new_top = (top - swapped(bottom)) * mask
    new_bottom = (bottom + swapped(top)) * mask
    return jnp.concatenate([new_top, new_bottom], axis=0).astype(jnp.bfloat16)


def forward_kernel(spec_ref, v_ref, u_ref, mask_ref, out_ref, rows):
    chunks, group, _ = spec_ref.shape
    tiles_row, tiles_col, _, rank_cap, tile_len = v_ref.shape[1:]
    owners = chunks // tiles_col
    sources = group // 4
    virtual = owners * sources
    for n in range(chunks):
        rows[n * group : (n + 1) * group, :] = spec_ref[n].astype(jnp.float32)
    products = []
    for b in range(tiles_col):
        spectra = jnp.concatenate(
            [
                jnp.concatenate(
                    [
                        rows[
                            pl.ds(b * group + h * 2 * sources + i, owners, stride=tiles_col * group),
                            :,
                        ]
                        for i in range(2 * sources)
                    ],
                    axis=0,
                )
                for h in range(2)
            ],
            axis=1,
        ).astype(jnp.bfloat16)
        bases = v_ref[0, :, b].reshape(tiles_row * 2 * rank_cap, tile_len)
        products.append(contract_last(spectra, bases))
    lane = lax.broadcasted_iota(jnp.int32, (2 * virtual, LANES), 1)
    nothing = jnp.zeros((2 * virtual, LANES), jnp.bfloat16)
    for p in range(tiles_row // 2):
        lanes = slice(p * LANES, (p + 1) * LANES)
        evens, odds = [], []
        for b in range(tiles_col):
            both = combined(
                products[b][:virtual, lanes],
                products[b][virtual:, lanes],
                mask_ref[b : b + 1, lanes],
            )
            evens.append(jnp.where(lane < 64, both, nothing))
            odds.append(jnp.where(lane < 64, nothing, both))
        left = jnp.concatenate(
            [jnp.concatenate(evens, axis=1), jnp.concatenate(odds, axis=1)], axis=0
        )
        bases = jnp.concatenate(
            [
                u_ref[0, 2 * p + i, b].reshape(2 * rank_cap, tile_len)
                for b in range(tiles_col)
                for i in range(2)
            ],
            axis=0,
        )
        terms = jnp.dot(left, bases, preferred_element_type=jnp.float32).astype(jnp.bfloat16)
        for i in range(2):
            for h in range(2):
                out_ref[2 * (2 * p + i) + h] = terms[
                    i * 2 * virtual : (i + 1) * 2 * virtual, h * LANES : (h + 1) * LANES
                ]


def sum_kernel(sources, parts_ref, out_ref, rows):
    count, height, _ = parts_ref.shape
    total = parts_ref[0].astype(jnp.float32)
    for n in range(1, count):
        total = total + parts_ref[n].astype(jnp.float32)
    virtual = height // 2
    owners = virtual // sources
    for c in range(2):
        for g in range(sources):
            start = c * virtual + g * owners
            rows[pl.ds(c * virtual + g, owners, stride=sources), :] = total[start : start + owners]
    piece = rows[...].astype(jnp.bfloat16)
    for n in range(count):
        out_ref[n] = piece


def adjoint_kernel(
    sources,
    observed_ref,
    total_ref,
    u_ref,
    v_ref,
    mask_ref,
    residual_ref,
    out_ref,
    rows,
    ordered,
    sems,
):
    chunks, group, _ = out_ref.shape
    tiles_row, tiles_col, _, rank_cap, tile_len = u_ref.shape[1:]
    virtual = observed_ref.shape[2]
    owners = chunks // tiles_col
    width = tiles_col * 2 * rank_cap
    pairs = width // LANES
    lane = lax.broadcasted_iota(jnp.int32, (2 * virtual, LANES), 1)
    nothing = jnp.zeros((2 * virtual, LANES), jnp.bfloat16)
    firsts = [[] for _ in range(pairs)]
    seconds = [[] for _ in range(pairs)]
    copies = []
    for a in range(tiles_row):
        data = []
        for h in range(2):
            n = 2 * a + h
            lanes = slice(n * LANES, (n + 1) * LANES)
            predicted = total_ref[n].astype(jnp.float32)
            parts = []
            for c in range(2):
                left = observed_ref[0, c, :, lanes] - predicted[c * virtual : (c + 1) * virtual]
                residual_ref[0, c, :, lanes] = left
                parts.append(left.astype(jnp.bfloat16))
            data.append(jnp.concatenate(parts, axis=0))
        products = contract_last(
            jnp.concatenate(data, axis=1), u_ref[0, a].reshape(width, tile_len)
        )
        for h in range(pairs):
            lanes = slice(h * LANES, (h + 1) * LANES)
            both = combined(
                products[:virtual, lanes], products[virtual:, lanes], mask_ref[a : a + 1, lanes]
            )
            firsts[h].append(jnp.where(lane < 64, both, nothing))
            seconds[h].append(jnp.where(lane < 64, nothing, both))
    for h in range(pairs):
        left = jnp.concatenate(
            [jnp.concatenate(firsts[h], axis=1), jnp.concatenate(seconds[h], axis=1)], axis=0
        )
        bases = v_ref[0, :, 2 * h : 2 * h + 2].reshape(tiles_row * LANES, tile_len)
        terms = jnp.dot(left, bases, preferred_element_type=jnp.float32)
        for k in range(2):
            rows[k, h * 4 * virtual : (h + 1) * 4 * virtual, :] = terms[:, k * LANES : (k + 1) * LANES]
    for b in range(tiles_col):
        for h in range(2):
            for c in range(2):
                for g in range(sources):
                    ordered[
                        pl.ds(
                            b * group + (h * 2 + c) * sources + g, owners, stride=tiles_col * group
                        ),
                        :,
                    ] = rows[h, pl.ds((b * 2 + c) * virtual + g, owners, stride=sources), :]
    for n in range(chunks):
        out_ref[n] = ordered[n * group : (n + 1) * group, :].astype(jnp.bfloat16)
    for copy in copies:
        copy.wait()


def back_kernel(
    scale, copies_in, residual_ref, parts_ref, basis_ref, residual_hbm, out_hbm, rows, held, sems
):
    pieces = held.shape[0]
    kept = pltpu.make_async_copy(residual_ref, residual_hbm, sems.at[pieces])
    kept.start()
    chunks, group, _ = parts_ref.shape
    freq_count = chunks // copies_in
    sources = group // 4
    for f in range(freq_count):
        total = parts_ref[f * copies_in].astype(jnp.float32)
        for r in range(1, copies_in):
            total = total + parts_ref[f * copies_in + r].astype(jnp.float32)
        rows[f * group : (f + 1) * group, :] = total
    basis = basis_ref[...]
    copies = [kept]
    for g in range(sources):
        for h in range(2):
            spectra = jnp.concatenate(
                [
                    rows[pl.ds((h * 2 + c) * sources + g, freq_count, stride=group), :]
                    for c in range(2)
                ],
                axis=0,
            ).astype(jnp.bfloat16)
            values = lax.dot_general(
                spectra, basis, (((0,), (0,)), ((), ())), preferred_element_type=jnp.float32
            )
            held[g * 2 + h] = (values * scale).astype(jnp.bfloat16)
            copy = pltpu.make_async_copy(
                held.at[g * 2 + h],
                out_hbm.at[g, 0, pl.ds(h * LANES, LANES)],
                sems.at[g * 2 + h],
            )
            copy.start()
            copies.append(copy)
    for copy in copies:
        copy.wait()


def spectrum_chunks(traces, u_bases, v_bases, ranks, freq_count, row_shards):
    sources, _, positions, trace_len = traces.shape
    tiles_row, tiles_col, _, rank_cap, _ = u_bases.shape[1:]
    halves = positions // LANES
    group = halves * 2 * sources
    return pl.pallas_call(
        lambda *refs: spectrum_kernel(1.0 / math.sqrt(trace_len), row_shards, *refs),
        out_shape=(
            jax.ShapeDtypeStruct((freq_count * row_shards, group, LANES), jnp.bfloat16),
            jax.ShapeDtypeStruct((2 * freq_count, trace_len), jnp.bfloat16),
            jax.ShapeDtypeStruct(u_bases.shape, jnp.bfloat16),
            jax.ShapeDtypeStruct(v_bases.shape, jnp.bfloat16),
            jax.ShapeDtypeStruct((tiles_row, tiles_col * 2 * rank_cap), jnp.float32),
            jax.ShapeDtypeStruct((tiles_col, tiles_row * 2 * rank_cap), jnp.float32),
        ),
        in_specs=[hbm_spec()] * 4,
        out_specs=(vmem_spec(),) * 6,
        scratch_shapes=[
            pltpu.VMEM((sources * halves, LANES, trace_len), jnp.bfloat16),
            pltpu.VMEM((freq_count * group, LANES), jnp.float32),
            pltpu.SMEM((tiles_col, tiles_row), jnp.int32),
            pltpu.SemaphoreType.DMA((3 + sources * halves,)),
        ],
        compiler_params=params(),
        cost_estimate=cost(
            2 * 2 * freq_count * traces.size, 2 * (traces.size + 2 * u_bases.size + 2 * v_bases.size)
        ),
        name="spectrum",
    )(in_hbm(traces), in_hbm(u_bases), in_hbm(v_bases), in_hbm(ranks))


def forward_chunks(spectra, v_bases, u_bases, mask, virtual):
    tiles_row = u_bases.shape[1]
    return pl.pallas_call(
        forward_kernel,
        out_shape=jax.ShapeDtypeStruct((2 * tiles_row, 2 * virtual, LANES), jnp.bfloat16),
        in_specs=[vmem_spec()] * 4,
        out_specs=vmem_spec(),
        scratch_shapes=[
            pltpu.VMEM((spectra.shape[0] * spectra.shape[1], LANES), jnp.float32),
        ],
        compiler_params=params(),
        cost_estimate=cost(8 * virtual * u_bases.size, 4 * u_bases.size),
        name="forward",
    )(spectra, v_bases, u_bases, mask)


def summed_chunks(parts, sources):
    return pl.pallas_call(
        lambda *refs: sum_kernel(sources, *refs),
        out_shape=jax.ShapeDtypeStruct(parts.shape, jnp.bfloat16),
        in_specs=[vmem_spec()],
        out_specs=vmem_spec(),
        scratch_shapes=[pltpu.VMEM(parts.shape[1:], jnp.float32)],
        compiler_params=params(),
        cost_estimate=cost(parts.size, 4 * parts.size),
        name="total",
    )(parts)


def adjoint_chunks(observed, total, u_bases, v_bases, mask, sources):
    tiles_col = u_bases.shape[2]
    tile_len = u_bases.shape[5]
    virtual = observed.shape[2]
    group = 4 * sources
    chunks = tiles_col * virtual // sources
    return pl.pallas_call(
        lambda *refs: adjoint_kernel(sources, *refs),
        out_shape=(
            jax.ShapeDtypeStruct(observed.shape, jnp.float32),
            jax.ShapeDtypeStruct((chunks, group, LANES), jnp.bfloat16),
        ),
        in_specs=[vmem_spec()] * 5,
        out_specs=(vmem_spec(), vmem_spec()),
        scratch_shapes=[
            pltpu.VMEM((tile_len // LANES, tiles_col * 2 * virtual, LANES), jnp.float32),
            pltpu.VMEM((chunks * group, LANES), jnp.float32),
            pltpu.SemaphoreType.DMA((u_bases.shape[1] // 4,)),
        ],
        compiler_params=params(),
        cost_estimate=cost(8 * virtual * u_bases.size, 4 * u_bases.size),
        name="adjoint",
    )(observed, total, u_bases, v_bases, mask)


def back_traces(residual, parts, basis, row_shards, shape):
    freq_count = basis.shape[0] // 2
    group = parts.shape[1]
    pieces = shape[0] * shape[2] // LANES
    return pl.pallas_call(
        lambda *refs: back_kernel(1.0 / math.sqrt(freq_count), row_shards, *refs),
        out_shape=(
            jax.ShapeDtypeStruct(residual.shape, jnp.float32),
            jax.ShapeDtypeStruct(shape, jnp.bfloat16),
        ),
        in_specs=[vmem_spec()] * 3,
        out_specs=(hbm_spec(), hbm_spec()),
        scratch_shapes=[
            pltpu.VMEM((freq_count * group, LANES), jnp.float32),
            pltpu.VMEM((pieces, LANES, shape[3]), jnp.bfloat16),
            pltpu.SemaphoreType.DMA((pieces + 1,)),
        ],
        compiler_params=params(),
        cost_estimate=cost(4 * freq_count * math.prod(shape), 2 * math.prod(shape)),
        name="back",
    )(residual, parts, basis)


def shards(traces, u_bases, v_bases, ranks, observed):
    virtual = observed.shape[2]
    sources = traces.shape[0]
    freq_count = u_bases.shape[0] * lax.axis_size("freq")
    row_shards = lax.axis_size("trow")

    def exchange(chunks, axes):
        return lax.all_to_all(chunks, axes, split_axis=0, concat_axis=0, tiled=True)

    spectra, basis, u_held, v_held, by_row, by_col = spectrum_chunks(
        traces, u_bases, v_bases, ranks[0].T, freq_count, row_shards
    )
    spectra = exchange(spectra, ("freq", "trow"))
    terms = exchange(forward_chunks(spectra, v_held, u_held, by_col, virtual), "tcol")
    total = exchange(summed_chunks(terms, sources), "tcol")
    residual, back = adjoint_chunks(observed, total, u_held, v_held, by_row, sources)
    back = exchange(back, ("freq", "trow"))
    return back_traces(residual, back, basis, row_shards, traces.shape)


def solution(mesh):
    placed = (
        P("freq", "tcol", "trow", None),
        P("freq", "trow", "tcol", None, None, None),
        P("freq", "trow", "tcol", None, None, None),
        P("freq", "trow", "tcol"),
        P("freq", None, None, "trow"),
    )
    return jax.shard_map(
        shards,
        mesh=mesh,
        in_specs=placed,
        out_specs=(P("freq", None, None, "trow"), P("freq", "tcol", "trow", None)),
        check_vma=False,
    )
```

```python
import math

import jax
import jax.numpy as jnp
from jax import lax
from jax.experimental import pallas as pl
from jax.experimental.pallas import tpu as pltpu
from jax.sharding import PartitionSpec as P

FIRST_BIN = 40
LANES = 128
SUBLANES = 8
VMEM_LIMIT = 16 * 1024 * 1024


def dft_angles(freq_bins, time_steps, trace_len):
    phase_index = freq_bins * time_steps % trace_len
    return phase_index.astype(jnp.float32) * (2.0 * math.pi / trace_len)


def contract_last(left, right):
    return lax.dot_general(
        left, right, (((1,), (1,)), ((), ())), preferred_element_type=jnp.float32
    )


def vmem_spec():
    return pl.BlockSpec(memory_space=pltpu.VMEM)


def hbm_spec():
    return pl.BlockSpec(memory_space=pltpu.HBM)


def turned(count, first):
    return [(first + i) % count for i in range(count)]


def exchange_orders(freq_shards, row_shards, col_shards):
    blocks = [
        f * row_shards + r
        for f in turned(freq_shards, freq_shards - 1)
        for r in turned(row_shards, row_shards - 1)
    ]
    columns = [2 * y + core for core in (1, 0) for y in turned(col_shards // 2, col_shards // 4)]
    return blocks, columns


def in_hbm(array):
    return pltpu.with_memory_space_constraint(array, pltpu.HBM)


def params():
    return pltpu.CompilerParams(vmem_limit_bytes=VMEM_LIMIT)


def cost(flops, moved):
    return pl.CostEstimate(flops=flops, bytes_accessed=moved, transcendentals=0)


def spectrum_kernel(
    scale,
    order,
    traces_hbm,
    u_hbm,
    v_hbm,
    ranks_hbm,
    out_ref,
    basis_ref,
    u_ref,
    v_ref,
    by_row_ref,
    by_col_ref,
    held,
    rows,
    ranks_ref,
    sems,
):
    sources, _, positions, trace_len = traces_hbm.shape
    halves = positions // LANES
    freq_count = basis_ref.shape[0] // 2
    tiles_row, tiles_col, _, rank_cap, _ = u_ref.shape[1:]
    rank_copy = pltpu.make_async_copy(ranks_hbm, ranks_ref, sems.at[0])
    v_copy = pltpu.make_async_copy(v_hbm, v_ref, sems.at[1])
    u_copy = pltpu.make_async_copy(u_hbm, u_ref, sems.at[2])
    copies = []
    for g in range(sources):
        for h in range(halves):
            copies.append(
                pltpu.make_async_copy(
                    traces_hbm.at[g, 0, pl.ds(h * LANES, LANES)],
                    held.at[g * halves + h],
                    sems.at[3 + g * halves + h],
                )
            )
    for copy in copies:
        copy.start()
    rank_copy.start()
    v_copy.start()
    u_copy.start()

    row = lax.broadcasted_iota(jnp.int32, basis_ref.shape, 0)
    time = lax.broadcasted_iota(jnp.int32, basis_ref.shape, 1)
    angles = dft_angles(FIRST_BIN + row % freq_count, time, trace_len)
    basis_ref[...] = jnp.where(row < freq_count, jnp.cos(angles), -jnp.sin(angles)).astype(
        jnp.bfloat16
    )
    rank_copy.wait()
    lane = lax.broadcasted_iota(jnp.int32, (1, LANES), 1)
    rank = lane % rank_cap
    low = lane < 2 * rank_cap
    for a in range(tiles_row):
        for b in range(0, tiles_col, 2):
            cap = jnp.where(low, ranks_ref[b, a], ranks_ref[b + 1, a])
            lanes = slice(b * 2 * rank_cap, (b + 2) * 2 * rank_cap)
            by_row_ref[a : a + 1, lanes] = jnp.where(rank < cap, 1.0, 0.0)
    for b in range(tiles_col):
        for a in range(0, tiles_row, 2):
            cap = jnp.where(low, ranks_ref[b, a], ranks_ref[b, a + 1])
            lanes = slice(a * 2 * rank_cap, (a + 2) * 2 * rank_cap)
            by_col_ref[b : b + 1, lanes] = jnp.where(rank < cap, 1.0, 0.0)

    group = halves * 2 * sources
    for copy in copies:
        copy.wait()
    spectra = (
        contract_last(basis_ref[...], held[...].reshape(sources * halves * LANES, trace_len))
        * scale
    )
    for g in range(sources):
        for h in range(halves):
            lanes = slice((g * halves + h) * LANES, (g * halves + h + 1) * LANES)
            for c in range(2):
                rows[pl.ds((h * 2 + c) * sources + g, freq_count, stride=group), :] = spectra[
                    c * freq_count : (c + 1) * freq_count, lanes
                ]
    copies_out = len(order) // freq_count
    for f in range(freq_count):
        piece = rows[f * group : (f + 1) * group, :].astype(jnp.bfloat16)
        for r in range(copies_out):
            out_ref[order.index(f * copies_out + r)] = piece
    v_copy.wait()
    u_copy.wait()


def combined(top, bottom, mask):
    lane = lax.broadcasted_iota(jnp.int32, top.shape, 1)
    first = (lane // 32) % 2 == 0

    def swapped(x):
        return jnp.where(
            first, -pltpu.roll(x, LANES - 32, 1), pltpu.roll(x, 32, 1)
        )

    new_top = (top - swapped(bottom)) * mask
    new_bottom = (bottom + swapped(top)) * mask
    return jnp.concatenate([new_top, new_bottom], axis=0).astype(jnp.bfloat16)


def forward_kernel(order, spec_ref, v_ref, u_ref, mask_ref, out_ref, rows):
    chunks, group, _ = spec_ref.shape
    tiles_row, tiles_col, _, rank_cap, tile_len = v_ref.shape[1:]
    owners = chunks // tiles_col
    sources = group // 4
    virtual = owners * sources
    for n in range(chunks):
        rows[order[n] * group : (order[n] + 1) * group, :] = spec_ref[n].astype(jnp.float32)
    products = []
    for b in range(tiles_col):
        spectra = jnp.concatenate(
            [
                jnp.concatenate(
                    [
                        rows[
                            pl.ds(b * group + h * 2 * sources + i, owners, stride=tiles_col * group),
                            :,
                        ]
                        for i in range(2 * sources)
                    ],
                    axis=0,
                )
                for h in range(2)
            ],
            axis=1,
        ).astype(jnp.bfloat16)
        bases = v_ref[0, :, b].reshape(tiles_row * 2 * rank_cap, tile_len)
        products.append(contract_last(spectra, bases))
    lane = lax.broadcasted_iota(jnp.int32, (2 * virtual, LANES), 1)
    nothing = jnp.zeros((2 * virtual, LANES), jnp.bfloat16)
    for p in range(tiles_row // 2):
        lanes = slice(p * LANES, (p + 1) * LANES)
        evens, odds = [], []
        for b in range(tiles_col):
            both = combined(
                products[b][:virtual, lanes],
                products[b][virtual:, lanes],
                mask_ref[b : b + 1, lanes],
            )
            evens.append(jnp.where(lane < 64, both, nothing))
            odds.append(jnp.where(lane < 64, nothing, both))
        left = jnp.concatenate(
            [jnp.concatenate(evens, axis=1), jnp.concatenate(odds, axis=1)], axis=0
        )
        bases = jnp.concatenate(
            [
                u_ref[0, 2 * p + i, b].reshape(2 * rank_cap, tile_len)
                for b in range(tiles_col)
                for i in range(2)
            ],
            axis=0,
        )
        terms = jnp.dot(left, bases, preferred_element_type=jnp.float32).astype(jnp.bfloat16)
        for i in range(2):
            for h in range(2):
                out_ref[2 * (2 * p + i) + h] = terms[
                    i * 2 * virtual : (i + 1) * 2 * virtual, h * LANES : (h + 1) * LANES
                ]


def sum_kernel(sources, parts_ref, out_ref, rows):
    count, height, _ = parts_ref.shape
    total = parts_ref[0].astype(jnp.float32)
    for n in range(1, count):
        total = total + parts_ref[n].astype(jnp.float32)
    virtual = height // 2
    owners = virtual // sources
    for c in range(2):
        for g in range(sources):
            start = c * virtual + g * owners
            rows[pl.ds(c * virtual + g, owners, stride=sources), :] = total[start : start + owners]
    piece = rows[...].astype(jnp.bfloat16)
    for n in range(count):
        out_ref[n] = piece


def adjoint_kernel(
    sources,
    order,
    observed_ref,
    total_ref,
    u_ref,
    v_ref,
    mask_ref,
    residual_ref,
    out_ref,
    rows,
    ordered,
    sems,
):
    chunks, group, _ = out_ref.shape
    tiles_row, tiles_col, _, rank_cap, tile_len = u_ref.shape[1:]
    virtual = observed_ref.shape[2]
    owners = chunks // tiles_col
    width = tiles_col * 2 * rank_cap
    pairs = width // LANES
    lane = lax.broadcasted_iota(jnp.int32, (2 * virtual, LANES), 1)
    nothing = jnp.zeros((2 * virtual, LANES), jnp.bfloat16)
    firsts = [[] for _ in range(pairs)]
    seconds = [[] for _ in range(pairs)]
    copies = []
    for a in range(tiles_row):
        data = []
        for h in range(2):
            n = 2 * a + h
            lanes = slice(n * LANES, (n + 1) * LANES)
            predicted = total_ref[n].astype(jnp.float32)
            parts = []
            for c in range(2):
                left = observed_ref[0, c, :, lanes] - predicted[c * virtual : (c + 1) * virtual]
                residual_ref[0, c, :, lanes] = left
                parts.append(left.astype(jnp.bfloat16))
            data.append(jnp.concatenate(parts, axis=0))
        products = contract_last(
            jnp.concatenate(data, axis=1), u_ref[0, a].reshape(width, tile_len)
        )
        for h in range(pairs):
            lanes = slice(h * LANES, (h + 1) * LANES)
            both = combined(
                products[:virtual, lanes], products[virtual:, lanes], mask_ref[a : a + 1, lanes]
            )
            firsts[h].append(jnp.where(lane < 64, both, nothing))
            seconds[h].append(jnp.where(lane < 64, nothing, both))
    for h in range(pairs):
        left = jnp.concatenate(
            [jnp.concatenate(firsts[h], axis=1), jnp.concatenate(seconds[h], axis=1)], axis=0
        )
        bases = v_ref[0, :, 2 * h : 2 * h + 2].reshape(tiles_row * LANES, tile_len)
        terms = jnp.dot(left, bases, preferred_element_type=jnp.float32)
        for k in range(2):
            rows[k, h * 4 * virtual : (h + 1) * 4 * virtual, :] = terms[:, k * LANES : (k + 1) * LANES]
    for b in range(tiles_col):
        for h in range(2):
            for c in range(2):
                for g in range(sources):
                    ordered[
                        pl.ds(
                            b * group + (h * 2 + c) * sources + g, owners, stride=tiles_col * group
                        ),
                        :,
                    ] = rows[h, pl.ds((b * 2 + c) * virtual + g, owners, stride=sources), :]
    for n in range(chunks):
        out_ref[n] = ordered[order[n] * group : (order[n] + 1) * group, :].astype(jnp.bfloat16)
    for copy in copies:
        copy.wait()


def back_kernel(
    scale, order, copies_in, residual_ref, parts_ref, basis_ref, residual_hbm, out_hbm, rows, held, sems
):
    pieces = held.shape[0]
    kept = pltpu.make_async_copy(residual_ref, residual_hbm, sems.at[pieces])
    kept.start()
    chunks, group, _ = parts_ref.shape
    freq_count = chunks // copies_in
    sources = group // 4
    for f in range(freq_count):
        total = parts_ref[order.index(f * copies_in)].astype(jnp.float32)
        for r in range(1, copies_in):
            total = total + parts_ref[order.index(f * copies_in + r)].astype(jnp.float32)
        rows[f * group : (f + 1) * group, :] = total
    basis = basis_ref[...]
    copies = [kept]
    for g in range(sources):
        for h in range(2):
            spectra = jnp.concatenate(
                [
                    rows[pl.ds((h * 2 + c) * sources + g, freq_count, stride=group), :]
                    for c in range(2)
                ],
                axis=0,
            ).astype(jnp.bfloat16)
            values = lax.dot_general(
                spectra, basis, (((0,), (0,)), ((), ())), preferred_element_type=jnp.float32
            )
            held[g * 2 + h] = (values * scale).astype(jnp.bfloat16)
            copy = pltpu.make_async_copy(
                held.at[g * 2 + h],
                out_hbm.at[g, 0, pl.ds(h * LANES, LANES)],
                sems.at[g * 2 + h],
            )
            copy.start()
            copies.append(copy)
    for copy in copies:
        copy.wait()


def spectrum_chunks(traces, u_bases, v_bases, ranks, freq_count, order):
    sources, _, positions, trace_len = traces.shape
    tiles_row, tiles_col, _, rank_cap, _ = u_bases.shape[1:]
    halves = positions // LANES
    group = halves * 2 * sources
    return pl.pallas_call(
        lambda *refs: spectrum_kernel(1.0 / math.sqrt(trace_len), order, *refs),
        out_shape=(
            jax.ShapeDtypeStruct((len(order), group, LANES), jnp.bfloat16),
            jax.ShapeDtypeStruct((2 * freq_count, trace_len), jnp.bfloat16),
            jax.ShapeDtypeStruct(u_bases.shape, jnp.bfloat16),
            jax.ShapeDtypeStruct(v_bases.shape, jnp.bfloat16),
            jax.ShapeDtypeStruct((tiles_row, tiles_col * 2 * rank_cap), jnp.float32),
            jax.ShapeDtypeStruct((tiles_col, tiles_row * 2 * rank_cap), jnp.float32),
        ),
        in_specs=[hbm_spec()] * 4,
        out_specs=(vmem_spec(),) * 6,
        scratch_shapes=[
            pltpu.VMEM((sources * halves, LANES, trace_len), jnp.bfloat16),
            pltpu.VMEM((freq_count * group, LANES), jnp.float32),
            pltpu.SMEM((tiles_col, tiles_row), jnp.int32),
            pltpu.SemaphoreType.DMA((3 + sources * halves,)),
        ],
        compiler_params=params(),
        cost_estimate=cost(
            2 * 2 * freq_count * traces.size, 2 * (traces.size + 2 * u_bases.size + 2 * v_bases.size)
        ),
        name="spectrum",
    )(in_hbm(traces), in_hbm(u_bases), in_hbm(v_bases), in_hbm(ranks))


def forward_chunks(spectra, v_bases, u_bases, mask, virtual, order):
    tiles_row = u_bases.shape[1]
    return pl.pallas_call(
        lambda *refs: forward_kernel(order, *refs),
        out_shape=jax.ShapeDtypeStruct((2 * tiles_row, 2 * virtual, LANES), jnp.bfloat16),
        in_specs=[vmem_spec()] * 4,
        out_specs=vmem_spec(),
        scratch_shapes=[
            pltpu.VMEM((spectra.shape[0] * spectra.shape[1], LANES), jnp.float32),
        ],
        compiler_params=params(),
        cost_estimate=cost(8 * virtual * u_bases.size, 4 * u_bases.size),
        name="forward",
    )(spectra, v_bases, u_bases, mask)


def summed_chunks(parts, sources):
    return pl.pallas_call(
        lambda *refs: sum_kernel(sources, *refs),
        out_shape=jax.ShapeDtypeStruct(parts.shape, jnp.bfloat16),
        in_specs=[vmem_spec()],
        out_specs=vmem_spec(),
        scratch_shapes=[pltpu.VMEM(parts.shape[1:], jnp.float32)],
        compiler_params=params(),
        cost_estimate=cost(parts.size, 4 * parts.size),
        name="total",
    )(parts)


def adjoint_chunks(observed, total, u_bases, v_bases, mask, sources, order):
    tiles_col = u_bases.shape[2]
    tile_len = u_bases.shape[5]
    virtual = observed.shape[2]
    group = 4 * sources
    chunks = tiles_col * virtual // sources
    return pl.pallas_call(
        lambda *refs: adjoint_kernel(sources, order, *refs),
        out_shape=(
            jax.ShapeDtypeStruct(observed.shape, jnp.float32),
            jax.ShapeDtypeStruct((chunks, group, LANES), jnp.bfloat16),
        ),
        in_specs=[vmem_spec()] * 5,
        out_specs=(vmem_spec(), vmem_spec()),
        scratch_shapes=[
            pltpu.VMEM((tile_len // LANES, tiles_col * 2 * virtual, LANES), jnp.float32),
            pltpu.VMEM((chunks * group, LANES), jnp.float32),
            pltpu.SemaphoreType.DMA((u_bases.shape[1] // 4,)),
        ],
        compiler_params=params(),
        cost_estimate=cost(8 * virtual * u_bases.size, 4 * u_bases.size),
        name="adjoint",
    )(observed, total, u_bases, v_bases, mask)


def back_traces(residual, parts, basis, row_shards, shape, order):
    freq_count = basis.shape[0] // 2
    group = parts.shape[1]
    pieces = shape[0] * shape[2] // LANES
    return pl.pallas_call(
        lambda *refs: back_kernel(1.0 / math.sqrt(freq_count), order, row_shards, *refs),
        out_shape=(
            jax.ShapeDtypeStruct(residual.shape, jnp.float32),
            jax.ShapeDtypeStruct(shape, jnp.bfloat16),
        ),
        in_specs=[vmem_spec()] * 3,
        out_specs=(hbm_spec(), hbm_spec()),
        scratch_shapes=[
            pltpu.VMEM((freq_count * group, LANES), jnp.float32),
            pltpu.VMEM((pieces, LANES, shape[3]), jnp.bfloat16),
            pltpu.SemaphoreType.DMA((pieces + 1,)),
        ],
        compiler_params=params(),
        cost_estimate=cost(4 * freq_count * math.prod(shape), 2 * math.prod(shape)),
        name="back",
    )(residual, parts, basis)


def shards(traces, u_bases, v_bases, ranks, observed):
    virtual = observed.shape[2]
    sources = traces.shape[0]
    freq_count = u_bases.shape[0] * lax.axis_size("freq")
    row_shards = lax.axis_size("trow")

    blocks, columns = exchange_orders(lax.axis_size("freq"), row_shards, lax.axis_size("tcol"))

    def exchange(chunks, axes, order):
        return lax.all_to_all(
            chunks, axes, split_axis=0, concat_axis=0, tiled=True, axis_index_groups=[order]
        )

    spectra, basis, u_held, v_held, by_row, by_col = spectrum_chunks(
        traces, u_bases, v_bases, ranks[0].T, freq_count, blocks
    )
    spectra = exchange(spectra, ("freq", "trow"), blocks)
    terms = forward_chunks(spectra, v_held, u_held, by_col, virtual, blocks)
    terms = exchange(terms, "tcol", columns)
    total = exchange(summed_chunks(terms, sources), "tcol", columns)
    residual, back = adjoint_chunks(observed, total, u_held, v_held, by_row, sources, blocks)
    back = exchange(back, ("freq", "trow"), blocks)
    return back_traces(residual, back, basis, row_shards, traces.shape, blocks)


def solution(mesh):
    placed = (
        P("freq", "tcol", "trow", None),
        P("freq", "trow", "tcol", None, None, None),
        P("freq", "trow", "tcol", None, None, None),
        P("freq", "trow", "tcol"),
        P("freq", None, None, "trow"),
    )
    return jax.shard_map(
        shards,
        mesh=mesh,
        in_specs=placed,
        out_specs=(P("freq", None, None, "trow"), P("freq", "tcol", "trow", None)),
        check_vma=False,
    )
```

```python
import math

import jax
import jax.numpy as jnp
from jax import lax
from jax.experimental import pallas as pl
from jax.experimental.pallas import tpu as pltpu
from jax.sharding import PartitionSpec as P

FIRST_BIN = 40
LANES = 128
SUBLANES = 8
VMEM_LIMIT = 16 * 1024 * 1024


def dft_angles(freq_bins, time_steps, trace_len):
    phase_index = freq_bins * time_steps % trace_len
    return phase_index.astype(jnp.float32) * (2.0 * math.pi / trace_len)


def contract_last(left, right):
    return lax.dot_general(
        left, right, (((1,), (1,)), ((), ())), preferred_element_type=jnp.float32
    )


def vmem_spec():
    return pl.BlockSpec(memory_space=pltpu.VMEM)


def hbm_spec():
    return pl.BlockSpec(memory_space=pltpu.HBM)


def turned(count, first):
    return [(first + i) % count for i in range(count)]


def exchange_orders(freq_shards, row_shards, col_shards):
    def blocks(first_row):
        return [
            f * row_shards + r
            for f in turned(freq_shards, freq_shards - 1)
            for r in turned(row_shards, first_row)
        ]

    columns = [2 * y + core for core in (1, 0) for y in turned(col_shards // 2, col_shards // 4)]
    return blocks(row_shards - 1), columns, blocks(row_shards // 2)


def in_hbm(array):
    return pltpu.with_memory_space_constraint(array, pltpu.HBM)


def params():
    return pltpu.CompilerParams(vmem_limit_bytes=VMEM_LIMIT)


def cost(flops, moved):
    return pl.CostEstimate(flops=flops, bytes_accessed=moved, transcendentals=0)


def spectrum_kernel(
    scale,
    order,
    traces_hbm,
    u_hbm,
    v_hbm,
    ranks_hbm,
    out_ref,
    basis_ref,
    u_ref,
    v_ref,
    by_row_ref,
    by_col_ref,
    held,
    rows,
    ranks_ref,
    sems,
):
    sources, _, positions, trace_len = traces_hbm.shape
    halves = positions // LANES
    freq_count = basis_ref.shape[0] // 2
    tiles_row, tiles_col, _, rank_cap, _ = u_ref.shape[1:]
    rank_copy = pltpu.make_async_copy(ranks_hbm, ranks_ref, sems.at[0])
    v_copy = pltpu.make_async_copy(v_hbm, v_ref, sems.at[1])
    u_copy = pltpu.make_async_copy(u_hbm, u_ref, sems.at[2])
    copies = []
    for g in range(sources):
        for h in range(halves):
            copies.append(
                pltpu.make_async_copy(
                    traces_hbm.at[g, 0, pl.ds(h * LANES, LANES)],
                    held.at[g * halves + h],
                    sems.at[3 + g * halves + h],
                )
            )
    for copy in copies:
        copy.start()
    rank_copy.start()
    v_copy.start()
    u_copy.start()

    row = lax.broadcasted_iota(jnp.int32, basis_ref.shape, 0)
    time = lax.broadcasted_iota(jnp.int32, basis_ref.shape, 1)
    angles = dft_angles(FIRST_BIN + row % freq_count, time, trace_len)
    basis_ref[...] = jnp.where(row < freq_count, jnp.cos(angles), -jnp.sin(angles)).astype(
        jnp.bfloat16
    )
    rank_copy.wait()
    lane = lax.broadcasted_iota(jnp.int32, (1, LANES), 1)
    rank = lane % rank_cap
    low = lane < 2 * rank_cap
    for a in range(tiles_row):
        for b in range(0, tiles_col, 2):
            cap = jnp.where(low, ranks_ref[b, a], ranks_ref[b + 1, a])
            lanes = slice(b * 2 * rank_cap, (b + 2) * 2 * rank_cap)
            by_row_ref[a : a + 1, lanes] = jnp.where(rank < cap, 1.0, 0.0)
    for b in range(tiles_col):
        for a in range(0, tiles_row, 2):
            cap = jnp.where(low, ranks_ref[b, a], ranks_ref[b, a + 1])
            lanes = slice(a * 2 * rank_cap, (a + 2) * 2 * rank_cap)
            by_col_ref[b : b + 1, lanes] = jnp.where(rank < cap, 1.0, 0.0)

    group = halves * 2 * sources
    for copy in copies:
        copy.wait()
    spectra = (
        contract_last(basis_ref[...], held[...].reshape(sources * halves * LANES, trace_len))
        * scale
    )
    for g in range(sources):
        for h in range(halves):
            lanes = slice((g * halves + h) * LANES, (g * halves + h + 1) * LANES)
            for c in range(2):
                rows[pl.ds((h * 2 + c) * sources + g, freq_count, stride=group), :] = spectra[
                    c * freq_count : (c + 1) * freq_count, lanes
                ]
    copies_out = len(order) // freq_count
    for f in range(freq_count):
        piece = rows[f * group : (f + 1) * group, :].astype(jnp.bfloat16)
        for r in range(copies_out):
            out_ref[order.index(f * copies_out + r)] = piece
    v_copy.wait()
    u_copy.wait()


def combined(top, bottom, mask):
    lane = lax.broadcasted_iota(jnp.int32, top.shape, 1)
    first = (lane // 32) % 2 == 0

    def swapped(x):
        return jnp.where(
            first, -pltpu.roll(x, LANES - 32, 1), pltpu.roll(x, 32, 1)
        )

    new_top = (top - swapped(bottom)) * mask
    new_bottom = (bottom + swapped(top)) * mask
    return jnp.concatenate([new_top, new_bottom], axis=0).astype(jnp.bfloat16)


def forward_kernel(order, spec_ref, v_ref, u_ref, mask_ref, out_ref, rows):
    chunks, group, _ = spec_ref.shape
    tiles_row, tiles_col, _, rank_cap, tile_len = v_ref.shape[1:]
    owners = chunks // tiles_col
    sources = group // 4
    virtual = owners * sources
    for n in range(chunks):
        rows[order[n] * group : (order[n] + 1) * group, :] = spec_ref[n].astype(jnp.float32)
    products = []
    for b in range(tiles_col):
        spectra = jnp.concatenate(
            [
                jnp.concatenate(
                    [
                        rows[
                            pl.ds(b * group + h * 2 * sources + i, owners, stride=tiles_col * group),
                            :,
                        ]
                        for i in range(2 * sources)
                    ],
                    axis=0,
                )
                for h in range(2)
            ],
            axis=1,
        ).astype(jnp.bfloat16)
        bases = v_ref[0, :, b].reshape(tiles_row * 2 * rank_cap, tile_len)
        products.append(contract_last(spectra, bases))
    lane = lax.broadcasted_iota(jnp.int32, (2 * virtual, LANES), 1)
    nothing = jnp.zeros((2 * virtual, LANES), jnp.bfloat16)
    for p in range(tiles_row // 2):
        lanes = slice(p * LANES, (p + 1) * LANES)
        evens, odds = [], []
        for b in range(tiles_col):
            both = combined(
                products[b][:virtual, lanes],
                products[b][virtual:, lanes],
                mask_ref[b : b + 1, lanes],
            )
            evens.append(jnp.where(lane < 64, both, nothing))
            odds.append(jnp.where(lane < 64, nothing, both))
        left = jnp.concatenate(
            [jnp.concatenate(evens, axis=1), jnp.concatenate(odds, axis=1)], axis=0
        )
        bases = jnp.concatenate(
            [
                u_ref[0, 2 * p + i, b].reshape(2 * rank_cap, tile_len)
                for b in range(tiles_col)
                for i in range(2)
            ],
            axis=0,
        )
        terms = jnp.dot(left, bases, preferred_element_type=jnp.float32).astype(jnp.bfloat16)
        for i in range(2):
            for h in range(2):
                out_ref[2 * (2 * p + i) + h] = terms[
                    i * 2 * virtual : (i + 1) * 2 * virtual, h * LANES : (h + 1) * LANES
                ]


def sum_kernel(sources, parts_ref, out_ref, rows):
    count, height, _ = parts_ref.shape
    total = parts_ref[0].astype(jnp.float32)
    for n in range(1, count):
        total = total + parts_ref[n].astype(jnp.float32)
    virtual = height // 2
    owners = virtual // sources
    for c in range(2):
        for g in range(sources):
            start = c * virtual + g * owners
            rows[pl.ds(c * virtual + g, owners, stride=sources), :] = total[start : start + owners]
    piece = rows[...].astype(jnp.bfloat16)
    for n in range(count):
        out_ref[n] = piece


def adjoint_kernel(
    sources,
    order,
    observed_ref,
    total_ref,
    u_ref,
    v_ref,
    mask_ref,
    residual_ref,
    out_ref,
    rows,
    ordered,
    sems,
):
    chunks, group, _ = out_ref.shape
    tiles_row, tiles_col, _, rank_cap, tile_len = u_ref.shape[1:]
    virtual = observed_ref.shape[2]
    owners = chunks // tiles_col
    width = tiles_col * 2 * rank_cap
    pairs = width // LANES
    lane = lax.broadcasted_iota(jnp.int32, (2 * virtual, LANES), 1)
    nothing = jnp.zeros((2 * virtual, LANES), jnp.bfloat16)
    firsts = [[] for _ in range(pairs)]
    seconds = [[] for _ in range(pairs)]
    copies = []
    for a in range(tiles_row):
        data = []
        for h in range(2):
            n = 2 * a + h
            lanes = slice(n * LANES, (n + 1) * LANES)
            predicted = total_ref[n].astype(jnp.float32)
            parts = []
            for c in range(2):
                left = observed_ref[0, c, :, lanes] - predicted[c * virtual : (c + 1) * virtual]
                residual_ref[0, c, :, lanes] = left
                parts.append(left.astype(jnp.bfloat16))
            data.append(jnp.concatenate(parts, axis=0))
        products = contract_last(
            jnp.concatenate(data, axis=1), u_ref[0, a].reshape(width, tile_len)
        )
        for h in range(pairs):
            lanes = slice(h * LANES, (h + 1) * LANES)
            both = combined(
                products[:virtual, lanes], products[virtual:, lanes], mask_ref[a : a + 1, lanes]
            )
            firsts[h].append(jnp.where(lane < 64, both, nothing))
            seconds[h].append(jnp.where(lane < 64, nothing, both))
    for h in range(pairs):
        left = jnp.concatenate(
            [jnp.concatenate(firsts[h], axis=1), jnp.concatenate(seconds[h], axis=1)], axis=0
        )
        bases = v_ref[0, :, 2 * h : 2 * h + 2].reshape(tiles_row * LANES, tile_len)
        terms = jnp.dot(left, bases, preferred_element_type=jnp.float32)
        for k in range(2):
            rows[k, h * 4 * virtual : (h + 1) * 4 * virtual, :] = terms[:, k * LANES : (k + 1) * LANES]
    for b in range(tiles_col):
        for h in range(2):
            for c in range(2):
                for g in range(sources):
                    ordered[
                        pl.ds(
                            b * group + (h * 2 + c) * sources + g, owners, stride=tiles_col * group
                        ),
                        :,
                    ] = rows[h, pl.ds((b * 2 + c) * virtual + g, owners, stride=sources), :]
    for n in range(chunks):
        out_ref[n] = ordered[order[n] * group : (order[n] + 1) * group, :].astype(jnp.bfloat16)
    for copy in copies:
        copy.wait()


def back_kernel(
    scale, order, copies_in, residual_ref, parts_ref, basis_ref, residual_hbm, out_hbm, rows, held, sems
):
    pieces = held.shape[0]
    kept = pltpu.make_async_copy(residual_ref, residual_hbm, sems.at[pieces])
    kept.start()
    chunks, group, _ = parts_ref.shape
    freq_count = chunks // copies_in
    sources = group // 4
    for f in range(freq_count):
        total = parts_ref[order.index(f * copies_in)].astype(jnp.float32)
        for r in range(1, copies_in):
            total = total + parts_ref[order.index(f * copies_in + r)].astype(jnp.float32)
        rows[f * group : (f + 1) * group, :] = total
    basis = basis_ref[...]
    copies = [kept]
    for g in range(sources):
        for h in range(2):
            spectra = jnp.concatenate(
                [
                    rows[pl.ds((h * 2 + c) * sources + g, freq_count, stride=group), :]
                    for c in range(2)
                ],
                axis=0,
            ).astype(jnp.bfloat16)
            values = lax.dot_general(
                spectra, basis, (((0,), (0,)), ((), ())), preferred_element_type=jnp.float32
            )
            held[g * 2 + h] = (values * scale).astype(jnp.bfloat16)
            copy = pltpu.make_async_copy(
                held.at[g * 2 + h],
                out_hbm.at[g, 0, pl.ds(h * LANES, LANES)],
                sems.at[g * 2 + h],
            )
            copy.start()
            copies.append(copy)
    for copy in copies:
        copy.wait()


def spectrum_chunks(traces, u_bases, v_bases, ranks, freq_count, order):
    sources, _, positions, trace_len = traces.shape
    tiles_row, tiles_col, _, rank_cap, _ = u_bases.shape[1:]
    halves = positions // LANES
    group = halves * 2 * sources
    return pl.pallas_call(
        lambda *refs: spectrum_kernel(1.0 / math.sqrt(trace_len), order, *refs),
        out_shape=(
            jax.ShapeDtypeStruct((len(order), group, LANES), jnp.bfloat16),
            jax.ShapeDtypeStruct((2 * freq_count, trace_len), jnp.bfloat16),
            jax.ShapeDtypeStruct(u_bases.shape, jnp.bfloat16),
            jax.ShapeDtypeStruct(v_bases.shape, jnp.bfloat16),
            jax.ShapeDtypeStruct((tiles_row, tiles_col * 2 * rank_cap), jnp.float32),
            jax.ShapeDtypeStruct((tiles_col, tiles_row * 2 * rank_cap), jnp.float32),
        ),
        in_specs=[hbm_spec()] * 4,
        out_specs=(vmem_spec(),) * 6,
        scratch_shapes=[
            pltpu.VMEM((sources * halves, LANES, trace_len), jnp.bfloat16),
            pltpu.VMEM((freq_count * group, LANES), jnp.float32),
            pltpu.SMEM((tiles_col, tiles_row), jnp.int32),
            pltpu.SemaphoreType.DMA((3 + sources * halves,)),
        ],
        compiler_params=params(),
        cost_estimate=cost(
            2 * 2 * freq_count * traces.size, 2 * (traces.size + 2 * u_bases.size + 2 * v_bases.size)
        ),
        name="spectrum",
    )(in_hbm(traces), in_hbm(u_bases), in_hbm(v_bases), in_hbm(ranks))


def forward_chunks(spectra, v_bases, u_bases, mask, virtual, order):
    tiles_row = u_bases.shape[1]
    return pl.pallas_call(
        lambda *refs: forward_kernel(order, *refs),
        out_shape=jax.ShapeDtypeStruct((2 * tiles_row, 2 * virtual, LANES), jnp.bfloat16),
        in_specs=[vmem_spec()] * 4,
        out_specs=vmem_spec(),
        scratch_shapes=[
            pltpu.VMEM((spectra.shape[0] * spectra.shape[1], LANES), jnp.float32),
        ],
        compiler_params=params(),
        cost_estimate=cost(8 * virtual * u_bases.size, 4 * u_bases.size),
        name="forward",
    )(spectra, v_bases, u_bases, mask)


def summed_chunks(parts, sources):
    return pl.pallas_call(
        lambda *refs: sum_kernel(sources, *refs),
        out_shape=jax.ShapeDtypeStruct(parts.shape, jnp.bfloat16),
        in_specs=[vmem_spec()],
        out_specs=vmem_spec(),
        scratch_shapes=[pltpu.VMEM(parts.shape[1:], jnp.float32)],
        compiler_params=params(),
        cost_estimate=cost(parts.size, 4 * parts.size),
        name="total",
    )(parts)


def adjoint_chunks(observed, total, u_bases, v_bases, mask, sources, order):
    tiles_col = u_bases.shape[2]
    tile_len = u_bases.shape[5]
    virtual = observed.shape[2]
    group = 4 * sources
    chunks = tiles_col * virtual // sources
    return pl.pallas_call(
        lambda *refs: adjoint_kernel(sources, order, *refs),
        out_shape=(
            jax.ShapeDtypeStruct(observed.shape, jnp.float32),
            jax.ShapeDtypeStruct((chunks, group, LANES), jnp.bfloat16),
        ),
        in_specs=[vmem_spec()] * 5,
        out_specs=(vmem_spec(), vmem_spec()),
        scratch_shapes=[
            pltpu.VMEM((tile_len // LANES, tiles_col * 2 * virtual, LANES), jnp.float32),
            pltpu.VMEM((chunks * group, LANES), jnp.float32),
            pltpu.SemaphoreType.DMA((u_bases.shape[1] // 4,)),
        ],
        compiler_params=params(),
        cost_estimate=cost(8 * virtual * u_bases.size, 4 * u_bases.size),
        name="adjoint",
    )(observed, total, u_bases, v_bases, mask)


def back_traces(residual, parts, basis, row_shards, shape, order):
    freq_count = basis.shape[0] // 2
    group = parts.shape[1]
    pieces = shape[0] * shape[2] // LANES
    return pl.pallas_call(
        lambda *refs: back_kernel(1.0 / math.sqrt(freq_count), order, row_shards, *refs),
        out_shape=(
            jax.ShapeDtypeStruct(residual.shape, jnp.float32),
            jax.ShapeDtypeStruct(shape, jnp.bfloat16),
        ),
        in_specs=[vmem_spec()] * 3,
        out_specs=(hbm_spec(), hbm_spec()),
        scratch_shapes=[
            pltpu.VMEM((freq_count * group, LANES), jnp.float32),
            pltpu.VMEM((pieces, LANES, shape[3]), jnp.bfloat16),
            pltpu.SemaphoreType.DMA((pieces + 1,)),
        ],
        compiler_params=params(),
        cost_estimate=cost(4 * freq_count * math.prod(shape), 2 * math.prod(shape)),
        name="back",
    )(residual, parts, basis)


def shards(traces, u_bases, v_bases, ranks, observed):
    virtual = observed.shape[2]
    sources = traces.shape[0]
    freq_count = u_bases.shape[0] * lax.axis_size("freq")
    row_shards = lax.axis_size("trow")

    outward, columns, homeward = exchange_orders(lax.axis_size("freq"), row_shards, lax.axis_size("tcol"))

    def exchange(chunks, axes, order):
        return lax.all_to_all(
            chunks, axes, split_axis=0, concat_axis=0, tiled=True, axis_index_groups=[order]
        )

    spectra, basis, u_held, v_held, by_row, by_col = spectrum_chunks(
        traces, u_bases, v_bases, ranks[0].T, freq_count, outward
    )
    spectra = exchange(spectra, ("freq", "trow"), outward)
    terms = forward_chunks(spectra, v_held, u_held, by_col, virtual, outward)
    terms = exchange(terms, "tcol", columns)
    total = exchange(summed_chunks(terms, sources), "tcol", columns)
    residual, back = adjoint_chunks(observed, total, u_held, v_held, by_row, sources, homeward)
    back = exchange(back, ("freq", "trow"), homeward)
    return back_traces(residual, back, basis, row_shards, traces.shape, homeward)


def solution(mesh):
    placed = (
        P("freq", "tcol", "trow", None),
        P("freq", "trow", "tcol", None, None, None),
        P("freq", "trow", "tcol", None, None, None),
        P("freq", "trow", "tcol"),
        P("freq", None, None, "trow"),
    )
    return jax.shard_map(
        shards,
        mesh=mesh,
        in_specs=placed,
        out_specs=(P("freq", None, None, "trow"), P("freq", "tcol", "trow", None)),
        check_vma=False,
    )
```

```python
import math

import jax
import jax.numpy as jnp
from jax import lax
from jax.experimental import pallas as pl
from jax.experimental.pallas import tpu as pltpu
from jax.sharding import PartitionSpec as P

FIRST_BIN = 40
LANES = 128
SUBLANES = 8
VMEM_LIMIT = 16 * 1024 * 1024


def dft_angles(freq_bins, time_steps, trace_len):
    phase_index = freq_bins * time_steps % trace_len
    return phase_index.astype(jnp.float32) * (2.0 * math.pi / trace_len)


def contract_last(left, right):
    return lax.dot_general(
        left, right, (((1,), (1,)), ((), ())), preferred_element_type=jnp.float32
    )


def vmem_spec():
    return pl.BlockSpec(memory_space=pltpu.VMEM)


def hbm_spec():
    return pl.BlockSpec(memory_space=pltpu.HBM)


def turned(count, first):
    return [(first + i) % count for i in range(count)]


def exchange_orders(freq_shards, row_shards, col_shards):
    def blocks(first_row):
        return [
            f * row_shards + r
            for f in turned(freq_shards, freq_shards - 1)
            for r in turned(row_shards, first_row)
        ]

    columns = [2 * y + core for core in (1, 0) for y in turned(col_shards // 2, col_shards // 4)]
    return blocks(row_shards - 1), columns, blocks(row_shards // 2)


def in_hbm(array):
    return pltpu.with_memory_space_constraint(array, pltpu.HBM)


def params():
    return pltpu.CompilerParams(vmem_limit_bytes=VMEM_LIMIT)


def cost(flops, moved):
    return pl.CostEstimate(flops=flops, bytes_accessed=moved, transcendentals=0)


def spectrum_kernel(
    scale,
    order,
    traces_hbm,
    u_hbm,
    v_hbm,
    ranks_hbm,
    out_ref,
    basis_ref,
    u_ref,
    v_ref,
    by_row_ref,
    by_col_ref,
    held,
    rows,
    ranks_ref,
    sems,
):
    sources, _, positions, trace_len = traces_hbm.shape
    halves = positions // LANES
    freq_count = basis_ref.shape[0] // 2
    tiles_row, tiles_col, _, rank_cap, _ = u_ref.shape[1:]
    rank_copy = pltpu.make_async_copy(ranks_hbm, ranks_ref, sems.at[0])
    v_copy = pltpu.make_async_copy(v_hbm, v_ref, sems.at[1])
    u_copy = pltpu.make_async_copy(u_hbm, u_ref, sems.at[2])
    copies = []
    for g in range(sources):
        for h in range(halves):
            copies.append(
                pltpu.make_async_copy(
                    traces_hbm.at[g, 0, pl.ds(h * LANES, LANES)],
                    held.at[g * halves + h],
                    sems.at[3 + g * halves + h],
                )
            )
    for copy in copies:
        copy.start()
    rank_copy.start()
    v_copy.start()
    u_copy.start()

    row = lax.broadcasted_iota(jnp.int32, basis_ref.shape, 0)
    time = lax.broadcasted_iota(jnp.int32, basis_ref.shape, 1)
    angles = dft_angles(FIRST_BIN + row % freq_count, time, trace_len)
    basis_ref[...] = jnp.where(row < freq_count, jnp.cos(angles), -jnp.sin(angles)).astype(
        jnp.bfloat16
    )
    rank_copy.wait()
    lane = lax.broadcasted_iota(jnp.int32, (1, LANES), 1)
    rank = lane % rank_cap
    low = lane < 2 * rank_cap
    for a in range(tiles_row):
        for b in range(0, tiles_col, 2):
            cap = jnp.where(low, ranks_ref[b, a], ranks_ref[b + 1, a])
            lanes = slice(b * 2 * rank_cap, (b + 2) * 2 * rank_cap)
            by_row_ref[a : a + 1, lanes] = jnp.where(rank < cap, 1.0, 0.0)
    for b in range(tiles_col):
        for a in range(0, tiles_row, 2):
            cap = jnp.where(low, ranks_ref[b, a], ranks_ref[b, a + 1])
            lanes = slice(a * 2 * rank_cap, (a + 2) * 2 * rank_cap)
            by_col_ref[b : b + 1, lanes] = jnp.where(rank < cap, 1.0, 0.0)

    group = halves * 2 * sources
    for copy in copies:
        copy.wait()
    spectra = (
        contract_last(basis_ref[...], held[...].reshape(sources * halves * LANES, trace_len))
        * scale
    )
    for g in range(sources):
        for h in range(halves):
            lanes = slice((g * halves + h) * LANES, (g * halves + h + 1) * LANES)
            for c in range(2):
                rows[pl.ds((h * 2 + c) * sources + g, freq_count, stride=group), :] = spectra[
                    c * freq_count : (c + 1) * freq_count, lanes
                ]
    copies_out = len(order) // freq_count
    for f in range(freq_count):
        piece = rows[f * group : (f + 1) * group, :].astype(jnp.bfloat16)
        for r in range(copies_out):
            out_ref[order.index(f * copies_out + r)] = piece
    v_copy.wait()
    u_copy.wait()


def combined(top, bottom, mask):
    lane = lax.broadcasted_iota(jnp.int32, top.shape, 1)
    first = (lane // 32) % 2 == 0

    def swapped(x):
        return jnp.where(
            first, -pltpu.roll(x, LANES - 32, 1), pltpu.roll(x, 32, 1)
        )

    new_top = (top - swapped(bottom)) * mask
    new_bottom = (bottom + swapped(top)) * mask
    return jnp.concatenate([new_top, new_bottom], axis=0).astype(jnp.bfloat16)


def forward_kernel(order, spec_ref, v_ref, u_ref, mask_ref, out_ref, rows):
    chunks, group, _ = spec_ref.shape
    tiles_row, tiles_col, _, rank_cap, tile_len = v_ref.shape[1:]
    owners = chunks // tiles_col
    sources = group // 4
    virtual = owners * sources
    for n in range(chunks):
        rows[order[n] * group : (order[n] + 1) * group, :] = spec_ref[n].astype(jnp.float32)
    products = []
    for b in range(tiles_col):
        spectra = jnp.concatenate(
            [
                jnp.concatenate(
                    [
                        rows[
                            pl.ds(b * group + h * 2 * sources + i, owners, stride=tiles_col * group),
                            :,
                        ]
                        for i in range(2 * sources)
                    ],
                    axis=0,
                )
                for h in range(2)
            ],
            axis=1,
        ).astype(jnp.bfloat16)
        bases = v_ref[0, :, b].reshape(tiles_row * 2 * rank_cap, tile_len)
        products.append(contract_last(spectra, bases))
    lane = lax.broadcasted_iota(jnp.int32, (2 * virtual, LANES), 1)
    nothing = jnp.zeros((2 * virtual, LANES), jnp.bfloat16)
    for p in range(tiles_row // 2):
        lanes = slice(p * LANES, (p + 1) * LANES)
        evens, odds = [], []
        for b in range(tiles_col):
            both = combined(
                products[b][:virtual, lanes],
                products[b][virtual:, lanes],
                mask_ref[b : b + 1, lanes],
            )
            evens.append(jnp.where(lane < 64, both, nothing))
            odds.append(jnp.where(lane < 64, nothing, both))
        left = jnp.concatenate(
            [jnp.concatenate(evens, axis=1), jnp.concatenate(odds, axis=1)], axis=0
        )
        bases = jnp.concatenate(
            [
                u_ref[0, 2 * p + i, b].reshape(2 * rank_cap, tile_len)
                for b in range(tiles_col)
                for i in range(2)
            ],
            axis=0,
        )
        terms = jnp.dot(left, bases, preferred_element_type=jnp.float32).astype(jnp.bfloat16)
        for i in range(2):
            for h in range(2):
                out_ref[2 * (2 * p + i) + h] = terms[
                    i * 2 * virtual : (i + 1) * 2 * virtual, h * LANES : (h + 1) * LANES
                ]


def sum_kernel(sources, parts_ref, out_ref, rows):
    count, height, _ = parts_ref.shape
    total = parts_ref[0].astype(jnp.float32)
    for n in range(1, count):
        total = total + parts_ref[n].astype(jnp.float32)
    virtual = height // 2
    owners = virtual // sources
    for c in range(2):
        for g in range(sources):
            start = c * virtual + g * owners
            rows[pl.ds(c * virtual + g, owners, stride=sources), :] = total[start : start + owners]
    piece = rows[:height, :].astype(jnp.bfloat16)
    for n in range(count):
        out_ref[n] = piece


def adjoint_kernel(
    sources,
    order,
    observed_ref,
    total_ref,
    u_ref,
    v_ref,
    mask_ref,
    residual_ref,
    out_ref,
    rows,
    ordered,
    sems,
):
    chunks, group, _ = out_ref.shape
    tiles_row, tiles_col, _, rank_cap, tile_len = u_ref.shape[1:]
    virtual = observed_ref.shape[2]
    owners = chunks // tiles_col
    width = tiles_col * 2 * rank_cap
    pairs = width // LANES
    lane = lax.broadcasted_iota(jnp.int32, (2 * virtual, LANES), 1)
    nothing = jnp.zeros((2 * virtual, LANES), jnp.bfloat16)
    firsts = [[] for _ in range(pairs)]
    seconds = [[] for _ in range(pairs)]
    copies = []
    for a in range(tiles_row):
        data = []
        for h in range(2):
            n = 2 * a + h
            lanes = slice(n * LANES, (n + 1) * LANES)
            predicted = total_ref[n].astype(jnp.float32)
            parts = []
            for c in range(2):
                left = observed_ref[0, c, :, lanes] - predicted[c * virtual : (c + 1) * virtual]
                residual_ref[0, c, :, lanes] = left
                parts.append(left.astype(jnp.bfloat16))
            data.append(jnp.concatenate(parts, axis=0))
        products = contract_last(
            jnp.concatenate(data, axis=1), u_ref[0, a].reshape(width, tile_len)
        )
        for h in range(pairs):
            lanes = slice(h * LANES, (h + 1) * LANES)
            both = combined(
                products[:virtual, lanes], products[virtual:, lanes], mask_ref[a : a + 1, lanes]
            )
            firsts[h].append(jnp.where(lane < 64, both, nothing))
            seconds[h].append(jnp.where(lane < 64, nothing, both))
    for h in range(pairs):
        left = jnp.concatenate(
            [jnp.concatenate(firsts[h], axis=1), jnp.concatenate(seconds[h], axis=1)], axis=0
        )
        bases = v_ref[0, :, 2 * h : 2 * h + 2].reshape(tiles_row * LANES, tile_len)
        terms = jnp.dot(left, bases, preferred_element_type=jnp.float32)
        for k in range(2):
            rows[k, h * 4 * virtual : (h + 1) * 4 * virtual, :] = terms[:, k * LANES : (k + 1) * LANES]
    for b in range(tiles_col):
        for h in range(2):
            for c in range(2):
                for g in range(sources):
                    ordered[
                        pl.ds(
                            b * group + (h * 2 + c) * sources + g, owners, stride=tiles_col * group
                        ),
                        :,
                    ] = rows[h, pl.ds((b * 2 + c) * virtual + g, owners, stride=sources), :]
    for n in range(chunks):
        out_ref[n] = ordered[order[n] * group : (order[n] + 1) * group, :].astype(jnp.bfloat16)
    for copy in copies:
        copy.wait()


def back_kernel(
    scale, order, copies_in, residual_ref, parts_ref, basis_ref, residual_hbm, out_hbm, rows, held, sems
):
    pieces = held.shape[0]
    kept = pltpu.make_async_copy(residual_ref, residual_hbm, sems.at[pieces])
    kept.start()
    chunks, group, _ = parts_ref.shape
    freq_count = chunks // copies_in
    sources = group // 4
    for f in range(freq_count):
        total = parts_ref[order.index(f * copies_in)].astype(jnp.float32)
        for r in range(1, copies_in):
            total = total + parts_ref[order.index(f * copies_in + r)].astype(jnp.float32)
        rows[f * group : (f + 1) * group, :] = total
    basis = basis_ref[...]
    copies = [kept]
    for g in range(sources):
        for h in range(2):
            spectra = jnp.concatenate(
                [
                    rows[pl.ds((h * 2 + c) * sources + g, freq_count, stride=group), :]
                    for c in range(2)
                ],
                axis=0,
            ).astype(jnp.bfloat16)
            values = lax.dot_general(
                spectra, basis, (((0,), (0,)), ((), ())), preferred_element_type=jnp.float32
            )
            held[g * 2 + h] = (values * scale).astype(jnp.bfloat16)
            copy = pltpu.make_async_copy(
                held.at[g * 2 + h],
                out_hbm.at[g, 0, pl.ds(h * LANES, LANES)],
                sems.at[g * 2 + h],
            )
            copy.start()
            copies.append(copy)
    for copy in copies:
        copy.wait()


def spectrum_chunks(traces, u_bases, v_bases, ranks, freq_count, order):
    sources, _, positions, trace_len = traces.shape
    tiles_row, tiles_col, _, rank_cap, _ = u_bases.shape[1:]
    halves = positions // LANES
    group = halves * 2 * sources
    return pl.pallas_call(
        lambda *refs: spectrum_kernel(1.0 / math.sqrt(trace_len), order, *refs),
        out_shape=(
            jax.ShapeDtypeStruct((len(order), group, LANES), jnp.bfloat16),
            jax.ShapeDtypeStruct((2 * freq_count, trace_len), jnp.bfloat16),
            jax.ShapeDtypeStruct(u_bases.shape, jnp.bfloat16),
            jax.ShapeDtypeStruct(v_bases.shape, jnp.bfloat16),
            jax.ShapeDtypeStruct((tiles_row, tiles_col * 2 * rank_cap), jnp.float32),
            jax.ShapeDtypeStruct((tiles_col, tiles_row * 2 * rank_cap), jnp.float32),
        ),
        in_specs=[hbm_spec()] * 4,
        out_specs=(vmem_spec(),) * 6,
        scratch_shapes=[
            pltpu.VMEM((sources * halves, LANES, trace_len), jnp.bfloat16),
            pltpu.VMEM(((freq_count + 1) * group, LANES), jnp.float32),
            pltpu.SMEM((tiles_col, tiles_row), jnp.int32),
            pltpu.SemaphoreType.DMA((3 + sources * halves,)),
        ],
        compiler_params=params(),
        cost_estimate=cost(
            2 * 2 * freq_count * traces.size, 2 * (traces.size + 2 * u_bases.size + 2 * v_bases.size)
        ),
        name="spectrum",
    )(in_hbm(traces), in_hbm(u_bases), in_hbm(v_bases), in_hbm(ranks))


def forward_chunks(spectra, v_bases, u_bases, mask, virtual, order):
    tiles_row = u_bases.shape[1]
    return pl.pallas_call(
        lambda *refs: forward_kernel(order, *refs),
        out_shape=jax.ShapeDtypeStruct((2 * tiles_row, 2 * virtual, LANES), jnp.bfloat16),
        in_specs=[vmem_spec()] * 4,
        out_specs=vmem_spec(),
        scratch_shapes=[
            pltpu.VMEM(((spectra.shape[0] + v_bases.shape[2]) * spectra.shape[1], LANES), jnp.float32),
        ],
        compiler_params=params(),
        cost_estimate=cost(8 * virtual * u_bases.size, 4 * u_bases.size),
        name="forward",
    )(spectra, v_bases, u_bases, mask)


def summed_chunks(parts, sources):
    return pl.pallas_call(
        lambda *refs: sum_kernel(sources, *refs),
        out_shape=jax.ShapeDtypeStruct(parts.shape, jnp.bfloat16),
        in_specs=[vmem_spec()],
        out_specs=vmem_spec(),
        scratch_shapes=[pltpu.VMEM((parts.shape[1] + SUBLANES, LANES), jnp.float32)],
        compiler_params=params(),
        cost_estimate=cost(parts.size, 4 * parts.size),
        name="total",
    )(parts)


def adjoint_chunks(observed, total, u_bases, v_bases, mask, sources, order):
    tiles_col = u_bases.shape[2]
    tile_len = u_bases.shape[5]
    virtual = observed.shape[2]
    group = 4 * sources
    chunks = tiles_col * virtual // sources
    return pl.pallas_call(
        lambda *refs: adjoint_kernel(sources, order, *refs),
        out_shape=(
            jax.ShapeDtypeStruct(observed.shape, jnp.float32),
            jax.ShapeDtypeStruct((chunks, group, LANES), jnp.bfloat16),
        ),
        in_specs=[vmem_spec()] * 5,
        out_specs=(vmem_spec(), vmem_spec()),
        scratch_shapes=[
            pltpu.VMEM((tile_len // LANES, tiles_col * 2 * virtual + SUBLANES, LANES), jnp.float32),
            pltpu.VMEM(((chunks + tiles_col) * group, LANES), jnp.float32),
            pltpu.SemaphoreType.DMA((u_bases.shape[1] // 4,)),
        ],
        compiler_params=params(),
        cost_estimate=cost(8 * virtual * u_bases.size, 4 * u_bases.size),
        name="adjoint",
    )(observed, total, u_bases, v_bases, mask)


def back_traces(residual, parts, basis, row_shards, shape, order):
    freq_count = basis.shape[0] // 2
    group = parts.shape[1]
    pieces = shape[0] * shape[2] // LANES
    return pl.pallas_call(
        lambda *refs: back_kernel(1.0 / math.sqrt(freq_count), order, row_shards, *refs),
        out_shape=(
            jax.ShapeDtypeStruct(residual.shape, jnp.float32),
            jax.ShapeDtypeStruct(shape, jnp.bfloat16),
        ),
        in_specs=[vmem_spec()] * 3,
        out_specs=(hbm_spec(), hbm_spec()),
        scratch_shapes=[
            pltpu.VMEM(((freq_count + 1) * group, LANES), jnp.float32),
            pltpu.VMEM((pieces, LANES, shape[3]), jnp.bfloat16),
            pltpu.SemaphoreType.DMA((pieces + 1,)),
        ],
        compiler_params=params(),
        cost_estimate=cost(4 * freq_count * math.prod(shape), 2 * math.prod(shape)),
        name="back",
    )(residual, parts, basis)


def shards(traces, u_bases, v_bases, ranks, observed):
    virtual = observed.shape[2]
    sources = traces.shape[0]
    freq_count = u_bases.shape[0] * lax.axis_size("freq")
    row_shards = lax.axis_size("trow")

    outward, columns, homeward = exchange_orders(
        lax.axis_size("freq"), row_shards, lax.axis_size("tcol")
    )

    def exchange(chunks, axes, order):
        return lax.all_to_all(
            chunks, axes, split_axis=0, concat_axis=0, tiled=True, axis_index_groups=[order]
        )

    spectra, basis, u_held, v_held, by_row, by_col = spectrum_chunks(
        traces, u_bases, v_bases, ranks[0].T, freq_count, outward
    )
    spectra = exchange(spectra, ("freq", "trow"), outward)
    terms = forward_chunks(spectra, v_held, u_held, by_col, virtual, outward)
    terms = exchange(terms, "tcol", columns)
    total = exchange(summed_chunks(terms, sources), "tcol", columns)
    residual, back = adjoint_chunks(observed, total, u_held, v_held, by_row, sources, homeward)
    back = exchange(back, ("freq", "trow"), homeward)
    return back_traces(residual, back, basis, row_shards, traces.shape, homeward)


def solution(mesh):
    placed = (
        P("freq", "tcol", "trow", None),
        P("freq", "trow", "tcol", None, None, None),
        P("freq", "trow", "tcol", None, None, None),
        P("freq", "trow", "tcol"),
        P("freq", None, None, "trow"),
    )
    return jax.shard_map(
        shards,
        mesh=mesh,
        in_specs=placed,
        out_specs=(P("freq", None, None, "trow"), P("freq", "tcol", "trow", None)),
        check_vma=False,
    )
```

```python
import math

import jax
import jax.numpy as jnp
from jax import lax
from jax.experimental import pallas as pl
from jax.experimental.pallas import tpu as pltpu
from jax.sharding import PartitionSpec as P

FIRST_BIN = 40
LANES = 128
SUBLANES = 8
VMEM_LIMIT = 16 * 1024 * 1024


def dft_angles(freq_bins, time_steps, trace_len):
    phase_index = freq_bins * time_steps % trace_len
    return phase_index.astype(jnp.float32) * (2.0 * math.pi / trace_len)


def contract_last(left, right):
    return lax.dot_general(
        left, right, (((1,), (1,)), ((), ())), preferred_element_type=jnp.float32
    )


def vmem_spec():
    return pl.BlockSpec(memory_space=pltpu.VMEM)


def hbm_spec():
    return pl.BlockSpec(memory_space=pltpu.HBM)


def turned(count, first):
    return [(first + i) % count for i in range(count)]


def exchange_orders(freq_shards, row_shards, col_shards):
    def blocks(first_row):
        return [
            f * row_shards + r
            for f in turned(freq_shards, freq_shards - 1)
            for r in turned(row_shards, first_row)
        ]

    chips = col_shards // 2
    columns = [2 * ((chips // 2 + 3 * i) % chips) + core for core in (1, 0) for i in range(chips)]
    return blocks(row_shards - 1), columns, blocks(row_shards // 2)


def in_hbm(array):
    return pltpu.with_memory_space_constraint(array, pltpu.HBM)


def params():
    return pltpu.CompilerParams(vmem_limit_bytes=VMEM_LIMIT)


def cost(flops, moved):
    return pl.CostEstimate(flops=flops, bytes_accessed=moved, transcendentals=0)


def spectrum_kernel(
    scale,
    order,
    traces_hbm,
    u_hbm,
    v_hbm,
    ranks_hbm,
    out_ref,
    basis_ref,
    u_ref,
    v_ref,
    by_row_ref,
    by_col_ref,
    held,
    rows,
    ranks_ref,
    sems,
):
    sources, _, positions, trace_len = traces_hbm.shape
    halves = positions // LANES
    freq_count = basis_ref.shape[0] // 2
    tiles_row, tiles_col, _, rank_cap, _ = u_ref.shape[1:]
    rank_copy = pltpu.make_async_copy(ranks_hbm, ranks_ref, sems.at[0])
    v_copy = pltpu.make_async_copy(v_hbm, v_ref, sems.at[1])
    u_copy = pltpu.make_async_copy(u_hbm, u_ref, sems.at[2])
    copies = []
    for g in range(sources):
        for h in range(halves):
            copies.append(
                pltpu.make_async_copy(
                    traces_hbm.at[g, 0, pl.ds(h * LANES, LANES)],
                    held.at[g * halves + h],
                    sems.at[3 + g * halves + h],
                )
            )
    for copy in copies:
        copy.start()
    rank_copy.start()
    v_copy.start()
    u_copy.start()

    row = lax.broadcasted_iota(jnp.int32, basis_ref.shape, 0)
    time = lax.broadcasted_iota(jnp.int32, basis_ref.shape, 1)
    angles = dft_angles(FIRST_BIN + row % freq_count, time, trace_len)
    basis_ref[...] = jnp.where(row < freq_count, jnp.cos(angles), -jnp.sin(angles)).astype(
        jnp.bfloat16
    )
    rank_copy.wait()
    lane = lax.broadcasted_iota(jnp.int32, (1, LANES), 1)
    rank = lane % rank_cap
    low = lane < 2 * rank_cap
    for a in range(tiles_row):
        for b in range(0, tiles_col, 2):
            cap = jnp.where(low, ranks_ref[b, a], ranks_ref[b + 1, a])
            lanes = slice(b * 2 * rank_cap, (b + 2) * 2 * rank_cap)
            by_row_ref[a : a + 1, lanes] = jnp.where(rank < cap, 1.0, 0.0)
    for b in range(tiles_col):
        for a in range(0, tiles_row, 2):
            cap = jnp.where(low, ranks_ref[b, a], ranks_ref[b, a + 1])
            lanes = slice(a * 2 * rank_cap, (a + 2) * 2 * rank_cap)
            by_col_ref[b : b + 1, lanes] = jnp.where(rank < cap, 1.0, 0.0)

    group = halves * 2 * sources
    for copy in copies:
        copy.wait()
    spectra = (
        contract_last(basis_ref[...], held[...].reshape(sources * halves * LANES, trace_len))
        * scale
    )
    for g in range(sources):
        for h in range(halves):
            lanes = slice((g * halves + h) * LANES, (g * halves + h + 1) * LANES)
            for c in range(2):
                rows[pl.ds((h * 2 + c) * sources + g, freq_count, stride=group), :] = spectra[
                    c * freq_count : (c + 1) * freq_count, lanes
                ]
    copies_out = len(order) // freq_count
    for f in range(freq_count):
        piece = rows[f * group : (f + 1) * group, :].astype(jnp.bfloat16)
        for r in range(copies_out):
            out_ref[order.index(f * copies_out + r)] = piece
    v_copy.wait()
    u_copy.wait()


def combined(top, bottom, mask):
    lane = lax.broadcasted_iota(jnp.int32, top.shape, 1)
    first = (lane // 32) % 2 == 0

    def swapped(x):
        return jnp.where(
            first, -pltpu.roll(x, LANES - 32, 1), pltpu.roll(x, 32, 1)
        )

    new_top = (top - swapped(bottom)) * mask
    new_bottom = (bottom + swapped(top)) * mask
    return jnp.concatenate([new_top, new_bottom], axis=0).astype(jnp.bfloat16)


def forward_kernel(order, spec_ref, v_ref, u_ref, mask_ref, out_ref, rows):
    chunks, group, _ = spec_ref.shape
    tiles_row, tiles_col, _, rank_cap, tile_len = v_ref.shape[1:]
    owners = chunks // tiles_col
    sources = group // 4
    virtual = owners * sources
    for n in range(chunks):
        rows[order[n] * group : (order[n] + 1) * group, :] = spec_ref[n].astype(jnp.float32)
    products = []
    for b in range(tiles_col):
        spectra = jnp.concatenate(
            [
                jnp.concatenate(
                    [
                        rows[
                            pl.ds(b * group + h * 2 * sources + i, owners, stride=tiles_col * group),
                            :,
                        ]
                        for i in range(2 * sources)
                    ],
                    axis=0,
                )
                for h in range(2)
            ],
            axis=1,
        ).astype(jnp.bfloat16)
        bases = v_ref[0, :, b].reshape(tiles_row * 2 * rank_cap, tile_len)
        products.append(contract_last(spectra, bases))
    lane = lax.broadcasted_iota(jnp.int32, (2 * virtual, LANES), 1)
    nothing = jnp.zeros((2 * virtual, LANES), jnp.bfloat16)
    for p in range(tiles_row // 2):
        lanes = slice(p * LANES, (p + 1) * LANES)
        evens, odds = [], []
        for b in range(tiles_col):
            both = combined(
                products[b][:virtual, lanes],
                products[b][virtual:, lanes],
                mask_ref[b : b + 1, lanes],
            )
            evens.append(jnp.where(lane < 64, both, nothing))
            odds.append(jnp.where(lane < 64, nothing, both))
        left = jnp.concatenate(
            [jnp.concatenate(evens, axis=1), jnp.concatenate(odds, axis=1)], axis=0
        )
        bases = jnp.concatenate(
            [
                u_ref[0, 2 * p + i, b].reshape(2 * rank_cap, tile_len)
                for b in range(tiles_col)
                for i in range(2)
            ],
            axis=0,
        )
        terms = jnp.dot(left, bases, preferred_element_type=jnp.float32).astype(jnp.bfloat16)
        for i in range(2):
            for h in range(2):
                out_ref[2 * (2 * p + i) + h] = terms[
                    i * 2 * virtual : (i + 1) * 2 * virtual, h * LANES : (h + 1) * LANES
                ]


def sum_kernel(sources, parts_ref, out_ref, rows):
    count, height, _ = parts_ref.shape
    total = parts_ref[0].astype(jnp.float32)
    for n in range(1, count):
        total = total + parts_ref[n].astype(jnp.float32)
    virtual = height // 2
    owners = virtual // sources
    for c in range(2):
        for g in range(sources):
            start = c * virtual + g * owners
            rows[pl.ds(c * virtual + g, owners, stride=sources), :] = total[start : start + owners]
    piece = rows[:height, :].astype(jnp.bfloat16)
    for n in range(count):
        out_ref[n] = piece


def adjoint_kernel(
    sources,
    order,
    observed_ref,
    total_ref,
    u_ref,
    v_ref,
    mask_ref,
    residual_ref,
    out_ref,
    rows,
    ordered,
    sems,
):
    chunks, group, _ = out_ref.shape
    tiles_row, tiles_col, _, rank_cap, tile_len = u_ref.shape[1:]
    virtual = observed_ref.shape[2]
    owners = chunks // tiles_col
    width = tiles_col * 2 * rank_cap
    pairs = width // LANES
    lane = lax.broadcasted_iota(jnp.int32, (2 * virtual, LANES), 1)
    nothing = jnp.zeros((2 * virtual, LANES), jnp.bfloat16)
    firsts = [[] for _ in range(pairs)]
    seconds = [[] for _ in range(pairs)]
    copies = []
    for a in range(tiles_row):
        data = []
        for h in range(2):
            n = 2 * a + h
            lanes = slice(n * LANES, (n + 1) * LANES)
            predicted = total_ref[n].astype(jnp.float32)
            parts = []
            for c in range(2):
                left = observed_ref[0, c, :, lanes] - predicted[c * virtual : (c + 1) * virtual]
                residual_ref[0, c, :, lanes] = left
                parts.append(left.astype(jnp.bfloat16))
            data.append(jnp.concatenate(parts, axis=0))
        products = contract_last(
            jnp.concatenate(data, axis=1), u_ref[0, a].reshape(width, tile_len)
        )
        for h in range(pairs):
            lanes = slice(h * LANES, (h + 1) * LANES)
            both = combined(
                products[:virtual, lanes], products[virtual:, lanes], mask_ref[a : a + 1, lanes]
            )
            firsts[h].append(jnp.where(lane < 64, both, nothing))
            seconds[h].append(jnp.where(lane < 64, nothing, both))
    for h in range(pairs):
        left = jnp.concatenate(
            [jnp.concatenate(firsts[h], axis=1), jnp.concatenate(seconds[h], axis=1)], axis=0
        )
        bases = v_ref[0, :, 2 * h : 2 * h + 2].reshape(tiles_row * LANES, tile_len)
        terms = jnp.dot(left, bases, preferred_element_type=jnp.float32)
        for k in range(2):
            rows[k, h * 4 * virtual : (h + 1) * 4 * virtual, :] = terms[:, k * LANES : (k + 1) * LANES]
    for b in range(tiles_col):
        for h in range(2):
            for c in range(2):
                for g in range(sources):
                    ordered[
                        pl.ds(
                            b * group + (h * 2 + c) * sources + g, owners, stride=tiles_col * group
                        ),
                        :,
                    ] = rows[h, pl.ds((b * 2 + c) * virtual + g, owners, stride=sources), :]
    for n in range(chunks):
        out_ref[n] = ordered[order[n] * group : (order[n] + 1) * group, :].astype(jnp.bfloat16)
    for copy in copies:
        copy.wait()


def back_kernel(
    scale, order, copies_in, residual_ref, parts_ref, basis_ref, residual_hbm, out_hbm, rows, held, sems
):
    pieces = held.shape[0]
    kept = pltpu.make_async_copy(residual_ref, residual_hbm, sems.at[pieces])
    kept.start()
    chunks, group, _ = parts_ref.shape
    freq_count = chunks // copies_in
    sources = group // 4
    for f in range(freq_count):
        total = parts_ref[order.index(f * copies_in)].astype(jnp.float32)
        for r in range(1, copies_in):
            total = total + parts_ref[order.index(f * copies_in + r)].astype(jnp.float32)
        rows[f * group : (f + 1) * group, :] = total
    basis = basis_ref[...]
    copies = [kept]
    for g in range(sources):
        for h in range(2):
            spectra = jnp.concatenate(
                [
                    rows[pl.ds((h * 2 + c) * sources + g, freq_count, stride=group), :]
                    for c in range(2)
                ],
                axis=0,
            ).astype(jnp.bfloat16)
            values = lax.dot_general(
                spectra, basis, (((0,), (0,)), ((), ())), preferred_element_type=jnp.float32
            )
            held[g * 2 + h] = (values * scale).astype(jnp.bfloat16)
            copy = pltpu.make_async_copy(
                held.at[g * 2 + h],
                out_hbm.at[g, 0, pl.ds(h * LANES, LANES)],
                sems.at[g * 2 + h],
            )
            copy.start()
            copies.append(copy)
    for copy in copies:
        copy.wait()


def spectrum_chunks(traces, u_bases, v_bases, ranks, freq_count, order):
    sources, _, positions, trace_len = traces.shape
    tiles_row, tiles_col, _, rank_cap, _ = u_bases.shape[1:]
    halves = positions // LANES
    group = halves * 2 * sources
    return pl.pallas_call(
        lambda *refs: spectrum_kernel(1.0 / math.sqrt(trace_len), order, *refs),
        out_shape=(
            jax.ShapeDtypeStruct((len(order), group, LANES), jnp.bfloat16),
            jax.ShapeDtypeStruct((2 * freq_count, trace_len), jnp.bfloat16),
            jax.ShapeDtypeStruct(u_bases.shape, jnp.bfloat16),
            jax.ShapeDtypeStruct(v_bases.shape, jnp.bfloat16),
            jax.ShapeDtypeStruct((tiles_row, tiles_col * 2 * rank_cap), jnp.float32),
            jax.ShapeDtypeStruct((tiles_col, tiles_row * 2 * rank_cap), jnp.float32),
        ),
        in_specs=[hbm_spec()] * 4,
        out_specs=(vmem_spec(),) * 6,
        scratch_shapes=[
            pltpu.VMEM((sources * halves, LANES, trace_len), jnp.bfloat16),
            pltpu.VMEM(((freq_count + 1) * group, LANES), jnp.float32),
            pltpu.SMEM((tiles_col, tiles_row), jnp.int32),
            pltpu.SemaphoreType.DMA((3 + sources * halves,)),
        ],
        compiler_params=params(),
        cost_estimate=cost(
            2 * 2 * freq_count * traces.size, 2 * (traces.size + 2 * u_bases.size + 2 * v_bases.size)
        ),
        name="spectrum",
    )(in_hbm(traces), in_hbm(u_bases), in_hbm(v_bases), in_hbm(ranks))


def forward_chunks(spectra, v_bases, u_bases, mask, virtual, order):
    tiles_row = u_bases.shape[1]
    return pl.pallas_call(
        lambda *refs: forward_kernel(order, *refs),
        out_shape=jax.ShapeDtypeStruct((2 * tiles_row, 2 * virtual, LANES), jnp.bfloat16),
        in_specs=[vmem_spec()] * 4,
        out_specs=vmem_spec(),
        scratch_shapes=[
            pltpu.VMEM(((spectra.shape[0] + v_bases.shape[2]) * spectra.shape[1], LANES), jnp.float32),
        ],
        compiler_params=params(),
        cost_estimate=cost(8 * virtual * u_bases.size, 4 * u_bases.size),
        name="forward",
    )(spectra, v_bases, u_bases, mask)


def summed_chunks(parts, sources):
    return pl.pallas_call(
        lambda *refs: sum_kernel(sources, *refs),
        out_shape=jax.ShapeDtypeStruct(parts.shape, jnp.bfloat16),
        in_specs=[vmem_spec()],
        out_specs=vmem_spec(),
        scratch_shapes=[pltpu.VMEM((parts.shape[1] + SUBLANES, LANES), jnp.float32)],
        compiler_params=params(),
        cost_estimate=cost(parts.size, 4 * parts.size),
        name="total",
    )(parts)


def adjoint_chunks(observed, total, u_bases, v_bases, mask, sources, order):
    tiles_col = u_bases.shape[2]
    tile_len = u_bases.shape[5]
    virtual = observed.shape[2]
    group = 4 * sources
    chunks = tiles_col * virtual // sources
    return pl.pallas_call(
        lambda *refs: adjoint_kernel(sources, order, *refs),
        out_shape=(
            jax.ShapeDtypeStruct(observed.shape, jnp.float32),
            jax.ShapeDtypeStruct((chunks, group, LANES), jnp.bfloat16),
        ),
        in_specs=[vmem_spec()] * 5,
        out_specs=(vmem_spec(), vmem_spec()),
        scratch_shapes=[
            pltpu.VMEM((tile_len // LANES, tiles_col * 2 * virtual + SUBLANES, LANES), jnp.float32),
            pltpu.VMEM(((chunks + tiles_col) * group, LANES), jnp.float32),
            pltpu.SemaphoreType.DMA((u_bases.shape[1] // 4,)),
        ],
        compiler_params=params(),
        cost_estimate=cost(8 * virtual * u_bases.size, 4 * u_bases.size),
        name="adjoint",
    )(observed, total, u_bases, v_bases, mask)


def back_traces(residual, parts, basis, row_shards, shape, order):
    freq_count = basis.shape[0] // 2
    group = parts.shape[1]
    pieces = shape[0] * shape[2] // LANES
    return pl.pallas_call(
        lambda *refs: back_kernel(1.0 / math.sqrt(freq_count), order, row_shards, *refs),
        out_shape=(
            jax.ShapeDtypeStruct(residual.shape, jnp.float32),
            jax.ShapeDtypeStruct(shape, jnp.bfloat16),
        ),
        in_specs=[vmem_spec()] * 3,
        out_specs=(hbm_spec(), hbm_spec()),
        scratch_shapes=[
            pltpu.VMEM(((freq_count + 1) * group, LANES), jnp.float32),
            pltpu.VMEM((pieces, LANES, shape[3]), jnp.bfloat16),
            pltpu.SemaphoreType.DMA((pieces + 1,)),
        ],
        compiler_params=params(),
        cost_estimate=cost(4 * freq_count * math.prod(shape), 2 * math.prod(shape)),
        name="back",
    )(residual, parts, basis)


def shards(traces, u_bases, v_bases, ranks, observed):
    virtual = observed.shape[2]
    sources = traces.shape[0]
    freq_count = u_bases.shape[0] * lax.axis_size("freq")
    row_shards = lax.axis_size("trow")

    outward, columns, homeward = exchange_orders(
        lax.axis_size("freq"), row_shards, lax.axis_size("tcol")
    )

    def exchange(chunks, axes, order):
        return lax.all_to_all(
            chunks, axes, split_axis=0, concat_axis=0, tiled=True, axis_index_groups=[order]
        )

    spectra, basis, u_held, v_held, by_row, by_col = spectrum_chunks(
        traces, u_bases, v_bases, ranks[0].T, freq_count, outward
    )
    spectra = exchange(spectra, ("freq", "trow"), outward)
    terms = forward_chunks(spectra, v_held, u_held, by_col, virtual, outward)
    terms = exchange(terms, "tcol", columns)
    total = exchange(summed_chunks(terms, sources), "tcol", columns)
    residual, back = adjoint_chunks(observed, total, u_held, v_held, by_row, sources, homeward)
    back = exchange(back, ("freq", "trow"), homeward)
    return back_traces(residual, back, basis, row_shards, traces.shape, homeward)


def solution(mesh):
    placed = (
        P("freq", "tcol", "trow", None),
        P("freq", "trow", "tcol", None, None, None),
        P("freq", "trow", "tcol", None, None, None),
        P("freq", "trow", "tcol"),
        P("freq", None, None, "trow"),
    )
    return jax.shard_map(
        shards,
        mesh=mesh,
        in_specs=placed,
        out_specs=(P("freq", None, None, "trow"), P("freq", "tcol", "trow", None)),
        check_vma=False,
    )
```

```python
import math

import jax
import jax.numpy as jnp
from jax import lax
from jax.experimental import pallas as pl
from jax.experimental.pallas import tpu as pltpu
from jax.sharding import PartitionSpec as P

FIRST_BIN = 40
LANES = 128
SUBLANES = 8
VMEM_LIMIT = 16 * 1024 * 1024


def dft_angles(freq_bins, time_steps, trace_len):
    phase_index = freq_bins * time_steps % trace_len
    return phase_index.astype(jnp.float32) * (2.0 * math.pi / trace_len)


def contract_last(left, right):
    return lax.dot_general(
        left, right, (((1,), (1,)), ((), ())), preferred_element_type=jnp.float32
    )


def vmem_spec():
    return pl.BlockSpec(memory_space=pltpu.VMEM)


def hbm_spec():
    return pl.BlockSpec(memory_space=pltpu.HBM)


def turned(count, first):
    return [(first + i) % count for i in range(count)]


def exchange_orders(freq_shards, row_shards, col_shards):
    def blocks(first_row):
        return [
            f * row_shards + r
            for f in turned(freq_shards, freq_shards - 1)
            for r in turned(row_shards, first_row)
        ]

    chips = col_shards // 2
    columns = [2 * ((chips // 2 + 3 * i) % chips) + core for core in (1, 0) for i in range(chips)]
    outward = [
        f * row_shards + r
        for r in turned(row_shards, row_shards - 1)
        for f in turned(freq_shards, freq_shards - 1)
    ]
    return outward, columns, blocks(row_shards // 2)


def in_hbm(array):
    return pltpu.with_memory_space_constraint(array, pltpu.HBM)


def params():
    return pltpu.CompilerParams(vmem_limit_bytes=VMEM_LIMIT)


def cost(flops, moved):
    return pl.CostEstimate(flops=flops, bytes_accessed=moved, transcendentals=0)


def spectrum_kernel(
    scale,
    order,
    traces_hbm,
    u_hbm,
    v_hbm,
    ranks_hbm,
    out_ref,
    basis_ref,
    u_ref,
    v_ref,
    by_row_ref,
    by_col_ref,
    held,
    rows,
    ranks_ref,
    sems,
):
    sources, _, positions, trace_len = traces_hbm.shape
    halves = positions // LANES
    freq_count = basis_ref.shape[0] // 2
    tiles_row, tiles_col, _, rank_cap, _ = u_ref.shape[1:]
    rank_copy = pltpu.make_async_copy(ranks_hbm, ranks_ref, sems.at[0])
    v_copy = pltpu.make_async_copy(v_hbm, v_ref, sems.at[1])
    u_copy = pltpu.make_async_copy(u_hbm, u_ref, sems.at[2])
    copies = []
    for g in range(sources):
        for h in range(halves):
            copies.append(
                pltpu.make_async_copy(
                    traces_hbm.at[g, 0, pl.ds(h * LANES, LANES)],
                    held.at[g * halves + h],
                    sems.at[3 + g * halves + h],
                )
            )
    for copy in copies:
        copy.start()
    rank_copy.start()
    v_copy.start()
    u_copy.start()

    row = lax.broadcasted_iota(jnp.int32, basis_ref.shape, 0)
    time = lax.broadcasted_iota(jnp.int32, basis_ref.shape, 1)
    angles = dft_angles(FIRST_BIN + row % freq_count, time, trace_len)
    basis_ref[...] = jnp.where(row < freq_count, jnp.cos(angles), -jnp.sin(angles)).astype(
        jnp.bfloat16
    )
    rank_copy.wait()
    lane = lax.broadcasted_iota(jnp.int32, (1, LANES), 1)
    rank = lane % rank_cap
    low = lane < 2 * rank_cap
    for a in range(tiles_row):
        for b in range(0, tiles_col, 2):
            cap = jnp.where(low, ranks_ref[b, a], ranks_ref[b + 1, a])
            lanes = slice(b * 2 * rank_cap, (b + 2) * 2 * rank_cap)
            by_row_ref[a : a + 1, lanes] = jnp.where(rank < cap, 1.0, 0.0)
    for b in range(tiles_col):
        for a in range(0, tiles_row, 2):
            cap = jnp.where(low, ranks_ref[b, a], ranks_ref[b, a + 1])
            lanes = slice(a * 2 * rank_cap, (a + 2) * 2 * rank_cap)
            by_col_ref[b : b + 1, lanes] = jnp.where(rank < cap, 1.0, 0.0)

    group = halves * 2 * sources
    for copy in copies:
        copy.wait()
    spectra = (
        contract_last(basis_ref[...], held[...].reshape(sources * halves * LANES, trace_len))
        * scale
    )
    for g in range(sources):
        for h in range(halves):
            lanes = slice((g * halves + h) * LANES, (g * halves + h + 1) * LANES)
            for c in range(2):
                rows[pl.ds((h * 2 + c) * sources + g, freq_count, stride=group), :] = spectra[
                    c * freq_count : (c + 1) * freq_count, lanes
                ]
    copies_out = len(order) // freq_count
    for f in range(freq_count):
        piece = rows[f * group : (f + 1) * group, :].astype(jnp.bfloat16)
        for r in range(copies_out):
            out_ref[order.index(f * copies_out + r)] = piece
    v_copy.wait()
    u_copy.wait()


def combined(top, bottom, mask):
    lane = lax.broadcasted_iota(jnp.int32, top.shape, 1)
    first = (lane // 32) % 2 == 0

    def swapped(x):
        return jnp.where(
            first, -pltpu.roll(x, LANES - 32, 1), pltpu.roll(x, 32, 1)
        )

    new_top = (top - swapped(bottom)) * mask
    new_bottom = (bottom + swapped(top)) * mask
    return jnp.concatenate([new_top, new_bottom], axis=0).astype(jnp.bfloat16)


def forward_kernel(order, spec_ref, v_ref, u_ref, mask_ref, out_ref, rows):
    chunks, group, _ = spec_ref.shape
    tiles_row, tiles_col, _, rank_cap, tile_len = v_ref.shape[1:]
    owners = chunks // tiles_col
    sources = group // 4
    virtual = owners * sources
    for n in range(chunks):
        rows[order[n] * group : (order[n] + 1) * group, :] = spec_ref[n].astype(jnp.float32)
    products = []
    for b in range(tiles_col):
        spectra = jnp.concatenate(
            [
                jnp.concatenate(
                    [
                        rows[
                            pl.ds(b * group + h * 2 * sources + i, owners, stride=tiles_col * group),
                            :,
                        ]
                        for i in range(2 * sources)
                    ],
                    axis=0,
                )
                for h in range(2)
            ],
            axis=1,
        ).astype(jnp.bfloat16)
        bases = v_ref[0, :, b].reshape(tiles_row * 2 * rank_cap, tile_len)
        products.append(contract_last(spectra, bases))
    lane = lax.broadcasted_iota(jnp.int32, (2 * virtual, LANES), 1)
    nothing = jnp.zeros((2 * virtual, LANES), jnp.bfloat16)
    for p in range(tiles_row // 2):
        lanes = slice(p * LANES, (p + 1) * LANES)
        evens, odds = [], []
        for b in range(tiles_col):
            both = combined(
                products[b][:virtual, lanes],
                products[b][virtual:, lanes],
                mask_ref[b : b + 1, lanes],
            )
            evens.append(jnp.where(lane < 64, both, nothing))
            odds.append(jnp.where(lane < 64, nothing, both))
        left = jnp.concatenate(
            [jnp.concatenate(evens, axis=1), jnp.concatenate(odds, axis=1)], axis=0
        )
        bases = jnp.concatenate(
            [
                u_ref[0, 2 * p + i, b].reshape(2 * rank_cap, tile_len)
                for b in range(tiles_col)
                for i in range(2)
            ],
            axis=0,
        )
        terms = jnp.dot(left, bases, preferred_element_type=jnp.float32).astype(jnp.bfloat16)
        for i in range(2):
            for h in range(2):
                out_ref[2 * (2 * p + i) + h] = terms[
                    i * 2 * virtual : (i + 1) * 2 * virtual, h * LANES : (h + 1) * LANES
                ]


def sum_kernel(sources, parts_ref, out_ref, rows):
    count, height, _ = parts_ref.shape
    total = parts_ref[0].astype(jnp.float32)
    for n in range(1, count):
        total = total + parts_ref[n].astype(jnp.float32)
    virtual = height // 2
    owners = virtual // sources
    for c in range(2):
        for g in range(sources):
            start = c * virtual + g * owners
            rows[pl.ds(c * virtual + g, owners, stride=sources), :] = total[start : start + owners]
    piece = rows[:height, :].astype(jnp.bfloat16)
    for n in range(count):
        out_ref[n] = piece


def adjoint_kernel(
    sources,
    order,
    observed_ref,
    total_ref,
    u_ref,
    v_ref,
    mask_ref,
    residual_ref,
    out_ref,
    rows,
    ordered,
    sems,
):
    chunks, group, _ = out_ref.shape
    tiles_row, tiles_col, _, rank_cap, tile_len = u_ref.shape[1:]
    virtual = observed_ref.shape[2]
    owners = chunks // tiles_col
    width = tiles_col * 2 * rank_cap
    pairs = width // LANES
    lane = lax.broadcasted_iota(jnp.int32, (2 * virtual, LANES), 1)
    nothing = jnp.zeros((2 * virtual, LANES), jnp.bfloat16)
    firsts = [[] for _ in range(pairs)]
    seconds = [[] for _ in range(pairs)]
    copies = []
    for a in range(tiles_row):
        data = []
        for h in range(2):
            n = 2 * a + h
            lanes = slice(n * LANES, (n + 1) * LANES)
            predicted = total_ref[n].astype(jnp.float32)
            parts = []
            for c in range(2):
                left = observed_ref[0, c, :, lanes] - predicted[c * virtual : (c + 1) * virtual]
                residual_ref[0, c, :, lanes] = left
                parts.append(left.astype(jnp.bfloat16))
            data.append(jnp.concatenate(parts, axis=0))
        products = contract_last(
            jnp.concatenate(data, axis=1), u_ref[0, a].reshape(width, tile_len)
        )
        for h in range(pairs):
            lanes = slice(h * LANES, (h + 1) * LANES)
            both = combined(
                products[:virtual, lanes], products[virtual:, lanes], mask_ref[a : a + 1, lanes]
            )
            firsts[h].append(jnp.where(lane < 64, both, nothing))
            seconds[h].append(jnp.where(lane < 64, nothing, both))
    for h in range(pairs):
        left = jnp.concatenate(
            [jnp.concatenate(firsts[h], axis=1), jnp.concatenate(seconds[h], axis=1)], axis=0
        )
        bases = v_ref[0, :, 2 * h : 2 * h + 2].reshape(tiles_row * LANES, tile_len)
        terms = jnp.dot(left, bases, preferred_element_type=jnp.float32)
        for k in range(2):
            rows[k, h * 4 * virtual : (h + 1) * 4 * virtual, :] = terms[:, k * LANES : (k + 1) * LANES]
    for b in range(tiles_col):
        for h in range(2):
            for c in range(2):
                for g in range(sources):
                    ordered[
                        pl.ds(
                            b * group + (h * 2 + c) * sources + g, owners, stride=tiles_col * group
                        ),
                        :,
                    ] = rows[h, pl.ds((b * 2 + c) * virtual + g, owners, stride=sources), :]
    for n in range(chunks):
        out_ref[n] = ordered[order[n] * group : (order[n] + 1) * group, :].astype(jnp.bfloat16)
    for copy in copies:
        copy.wait()


def back_kernel(
    scale, order, copies_in, residual_ref, parts_ref, basis_ref, residual_hbm, out_hbm, rows, held, sems
):
    pieces = held.shape[0]
    kept = pltpu.make_async_copy(residual_ref, residual_hbm, sems.at[pieces])
    kept.start()
    chunks, group, _ = parts_ref.shape
    freq_count = chunks // copies_in
    sources = group // 4
    for f in range(freq_count):
        total = parts_ref[order.index(f * copies_in)].astype(jnp.float32)
        for r in range(1, copies_in):
            total = total + parts_ref[order.index(f * copies_in + r)].astype(jnp.float32)
        rows[f * group : (f + 1) * group, :] = total
    basis = basis_ref[...]
    copies = [kept]
    for g in range(sources):
        for h in range(2):
            spectra = jnp.concatenate(
                [
                    rows[pl.ds((h * 2 + c) * sources + g, freq_count, stride=group), :]
                    for c in range(2)
                ],
                axis=0,
            ).astype(jnp.bfloat16)
            values = lax.dot_general(
                spectra, basis, (((0,), (0,)), ((), ())), preferred_element_type=jnp.float32
            )
            held[g * 2 + h] = (values * scale).astype(jnp.bfloat16)
            copy = pltpu.make_async_copy(
                held.at[g * 2 + h],
                out_hbm.at[g, 0, pl.ds(h * LANES, LANES)],
                sems.at[g * 2 + h],
            )
            copy.start()
            copies.append(copy)
    for copy in copies:
        copy.wait()


def spectrum_chunks(traces, u_bases, v_bases, ranks, freq_count, order):
    sources, _, positions, trace_len = traces.shape
    tiles_row, tiles_col, _, rank_cap, _ = u_bases.shape[1:]
    halves = positions // LANES
    group = halves * 2 * sources
    return pl.pallas_call(
        lambda *refs: spectrum_kernel(1.0 / math.sqrt(trace_len), order, *refs),
        out_shape=(
            jax.ShapeDtypeStruct((len(order), group, LANES), jnp.bfloat16),
            jax.ShapeDtypeStruct((2 * freq_count, trace_len), jnp.bfloat16),
            jax.ShapeDtypeStruct(u_bases.shape, jnp.bfloat16),
            jax.ShapeDtypeStruct(v_bases.shape, jnp.bfloat16),
            jax.ShapeDtypeStruct((tiles_row, tiles_col * 2 * rank_cap), jnp.float32),
            jax.ShapeDtypeStruct((tiles_col, tiles_row * 2 * rank_cap), jnp.float32),
        ),
        in_specs=[hbm_spec()] * 4,
        out_specs=(vmem_spec(),) * 6,
        scratch_shapes=[
            pltpu.VMEM((sources * halves, LANES, trace_len), jnp.bfloat16),
            pltpu.VMEM(((freq_count + 1) * group, LANES), jnp.float32),
            pltpu.SMEM((tiles_col, tiles_row), jnp.int32),
            pltpu.SemaphoreType.DMA((3 + sources * halves,)),
        ],
        compiler_params=params(),
        cost_estimate=cost(
            2 * 2 * freq_count * traces.size, 2 * (traces.size + 2 * u_bases.size + 2 * v_bases.size)
        ),
        name="spectrum",
    )(in_hbm(traces), in_hbm(u_bases), in_hbm(v_bases), in_hbm(ranks))


def forward_chunks(spectra, v_bases, u_bases, mask, virtual, order):
    tiles_row = u_bases.shape[1]
    return pl.pallas_call(
        lambda *refs: forward_kernel(order, *refs),
        out_shape=jax.ShapeDtypeStruct((2 * tiles_row, 2 * virtual, LANES), jnp.bfloat16),
        in_specs=[vmem_spec()] * 4,
        out_specs=vmem_spec(),
        scratch_shapes=[
            pltpu.VMEM(((spectra.shape[0] + v_bases.shape[2]) * spectra.shape[1], LANES), jnp.float32),
        ],
        compiler_params=params(),
        cost_estimate=cost(8 * virtual * u_bases.size, 4 * u_bases.size),
        name="forward",
    )(spectra, v_bases, u_bases, mask)


def summed_chunks(parts, sources):
    return pl.pallas_call(
        lambda *refs: sum_kernel(sources, *refs),
        out_shape=jax.ShapeDtypeStruct(parts.shape, jnp.bfloat16),
        in_specs=[vmem_spec()],
        out_specs=vmem_spec(),
        scratch_shapes=[pltpu.VMEM((parts.shape[1] + SUBLANES, LANES), jnp.float32)],
        compiler_params=params(),
        cost_estimate=cost(parts.size, 4 * parts.size),
        name="total",
    )(parts)


def adjoint_chunks(observed, total, u_bases, v_bases, mask, sources, order):
    tiles_col = u_bases.shape[2]
    tile_len = u_bases.shape[5]
    virtual = observed.shape[2]
    group = 4 * sources
    chunks = tiles_col * virtual // sources
    return pl.pallas_call(
        lambda *refs: adjoint_kernel(sources, order, *refs),
        out_shape=(
            jax.ShapeDtypeStruct(observed.shape, jnp.float32),
            jax.ShapeDtypeStruct((chunks, group, LANES), jnp.bfloat16),
        ),
        in_specs=[vmem_spec()] * 5,
        out_specs=(vmem_spec(), vmem_spec()),
        scratch_shapes=[
            pltpu.VMEM((tile_len // LANES, tiles_col * 2 * virtual + SUBLANES, LANES), jnp.float32),
            pltpu.VMEM(((chunks + tiles_col) * group, LANES), jnp.float32),
            pltpu.SemaphoreType.DMA((u_bases.shape[1] // 4,)),
        ],
        compiler_params=params(),
        cost_estimate=cost(8 * virtual * u_bases.size, 4 * u_bases.size),
        name="adjoint",
    )(observed, total, u_bases, v_bases, mask)


def back_traces(residual, parts, basis, row_shards, shape, order):
    freq_count = basis.shape[0] // 2
    group = parts.shape[1]
    pieces = shape[0] * shape[2] // LANES
    return pl.pallas_call(
        lambda *refs: back_kernel(1.0 / math.sqrt(freq_count), order, row_shards, *refs),
        out_shape=(
            jax.ShapeDtypeStruct(residual.shape, jnp.float32),
            jax.ShapeDtypeStruct(shape, jnp.bfloat16),
        ),
        in_specs=[vmem_spec()] * 3,
        out_specs=(hbm_spec(), hbm_spec()),
        scratch_shapes=[
            pltpu.VMEM(((freq_count + 1) * group, LANES), jnp.float32),
            pltpu.VMEM((pieces, LANES, shape[3]), jnp.bfloat16),
            pltpu.SemaphoreType.DMA((pieces + 1,)),
        ],
        compiler_params=params(),
        cost_estimate=cost(4 * freq_count * math.prod(shape), 2 * math.prod(shape)),
        name="back",
    )(residual, parts, basis)


def shards(traces, u_bases, v_bases, ranks, observed):
    virtual = observed.shape[2]
    sources = traces.shape[0]
    freq_count = u_bases.shape[0] * lax.axis_size("freq")
    row_shards = lax.axis_size("trow")

    outward, columns, homeward = exchange_orders(
        lax.axis_size("freq"), row_shards, lax.axis_size("tcol")
    )

    def exchange(chunks, axes, order):
        return lax.all_to_all(
            chunks, axes, split_axis=0, concat_axis=0, tiled=True, axis_index_groups=[order]
        )

    spectra, basis, u_held, v_held, by_row, by_col = spectrum_chunks(
        traces, u_bases, v_bases, ranks[0].T, freq_count, outward
    )
    spectra = exchange(spectra, ("freq", "trow"), outward)
    terms = forward_chunks(spectra, v_held, u_held, by_col, virtual, outward)
    terms = exchange(terms, "tcol", columns)
    total = exchange(summed_chunks(terms, sources), "tcol", columns)
    residual, back = adjoint_chunks(observed, total, u_held, v_held, by_row, sources, homeward)
    back = exchange(back, ("freq", "trow"), homeward)
    return back_traces(residual, back, basis, row_shards, traces.shape, homeward)


def solution(mesh):
    placed = (
        P("freq", "tcol", "trow", None),
        P("freq", "trow", "tcol", None, None, None),
        P("freq", "trow", "tcol", None, None, None),
        P("freq", "trow", "tcol"),
        P("freq", None, None, "trow"),
    )
    return jax.shard_map(
        shards,
        mesh=mesh,
        in_specs=placed,
        out_specs=(P("freq", None, None, "trow"), P("freq", "tcol", "trow", None)),
        check_vma=False,
    )
```
